256 devices in a mesh: island: 8 (over y_hi, x), fsdp: 32 (over y_lo, z, core).
Axes of the slice: x: 4, y: 4 (y_hi: 2, y_lo: 2; y = y_hi * 2 + y_lo), z: 8, core: 2. Of those that a mesh axis runs over, the one named last changes fastest.
Arguments:
- hidden_in: bfloat16 [8, 8192, 8192], P('island', 'fsdp'), may hold values from -6 to 6
- norm_gain: bfloat16 [8, 8192], P('island'), may hold values from 0.5 to 2
- key_weight: bfloat16 [8, 8192, 512], P('island', 'fsdp'), may hold values from -0.0625 to 0.0625
- key_cotangent: bfloat16 [8, 8192, 512], P('island', 'fsdp'), may hold values from -6 to 6
- frag_global: float32 [8192, 512], P('fsdp'), may hold values from -6 to 6
- frag_moment: float32 [8192, 512], P('fsdp'), may hold values from -4 to 4
- frag_local: bfloat16 [8, 8192, 512], P('island', 'fsdp'), may hold values from -6 to 6
Outputs:
- keys: bfloat16 [8, 8192, 512], P('island', 'fsdp')
- grad_in: bfloat16 [8, 8192, 8192], P('island', 'fsdp')
- grad_w: float32 [8, 8192, 512], P('island', 'fsdp')
- new_global: float32 [8192, 512], P('fsdp')
- new_moment: float32 [8192, 512], P('fsdp')
- new_local: bfloat16 [8, 8192, 512], P('island', 'fsdp')
The draws below stay inside these ranges and needn't reach their ends.
All inputs are finite; a program needn't handle non-finite values.
Results may differ from the reference program's by a relative error of at most 0.0049.
Values may be sent and summed in bfloat16 or wider, within the bound.
A program may use at most 128 MiB of HBM per device.

```python
import math
import jax
import jax.numpy as jnp
from jax import lax

D = 8192
TOK_DEV = 256
KC = 512
TOKENS = 8192
N_ISLAND = 8
N_FSDP = 32


def with_spikes(drawn, stream_key, source, target, blocks, factor):
    owner, partner = [(jnp.arange(drawn.shape[position]) // (drawn.shape[position] // blocks)).reshape([-1 if axis == position else 1 for axis in range(drawn.ndim)]) for position in (source, target)]
    chosen = jax.random.permutation(stream_key, blocks)[partner]
    strong = (owner == chosen) | (owner == (partner + blocks // 2) % blocks)
    return jnp.where(strong, factor * drawn, drawn)


def steps_of(key, extent, split, low, top_value):
    factor_of = 1.0
    for position, blocks in split:
        draws = jax.random.uniform(jax.random.fold_in(jax.random.fold_in(key, 6), position), (blocks,), jnp.float32, low / len(split), top_value / len(split))
        factor_of = factor_of * jnp.repeat(jnp.exp(draws), extent[position] // blocks).reshape((-1,) + (1,) * (len(extent) - 1 - position))
    return factor_of


def scatter_about(key, shape, scale, bound, pieces=(), held_as=jnp.bfloat16):
    values = scale * jax.random.normal(key, shape, jnp.float32)
    if pieces:
        values = values * steps_of(key, shape, pieces, -0.22, 0.18)
    return jnp.clip(values, -bound, bound).astype(held_as)


def heavy_noise(key, dims, width, limit, cuts, heavy, dtype=jnp.bfloat16):
    result = width * jax.random.normal(key, dims, jnp.float32)
    if cuts:
        result = result * steps_of(key, dims, cuts, -0.22, 0.18)
    return jnp.clip(with_spikes(result, jax.random.fold_in(key, 3), *heavy), -limit, limit).astype(dtype)


def setup_inputs(seed: int = 0) -> dict:
    splits = jax.random.split(jax.random.key(seed), 8)
    return {
        "hidden_in": heavy_noise(splits[0], (N_ISLAND, TOKENS, D), 1.0, 6.0, ((0, 8), (1, 32)), (1, 2, 32, 2.75)),
        "norm_gain": jnp.clip(jnp.exp(math.log(2.0) - 1.3862944 * jax.random.uniform(splits[1], (N_ISLAND, D), jnp.float32) ** steps_of(splits[1], (N_ISLAND, D), ((0, 8),), -0.2, 0.2)), 0.5, 2.0).astype(jnp.bfloat16),
        "key_weight": scatter_about(splits[2], (N_ISLAND, D, KC), D ** -0.5, 0.0625, ((0, 8), (1, 32))),
        "key_cotangent": scatter_about(splits[3], (N_ISLAND, TOKENS, KC), 1.0, 6.0, ((0, 8), (1, 32))),
        "frag_global": scatter_about(splits[4], (D, KC), 1.0, 6.0, ((0, 32),), jnp.float32),
        "frag_moment": scatter_about(splits[5], (D, KC), 0.5, 4.0, ((0, 32),), jnp.float32),
        "frag_local": scatter_about(splits[6], (N_ISLAND, D, KC), 1.0, 6.0, ((0, 8), (1, 32))),
    }


epsilon = 1e-05
outer_rate = 0.7
outer_momentum = 0.9
mix_weight = 0.5

def one_island(pack):
    hidden, gain, weight, cotangent = pack
    hidden_f = hidden.astype(jnp.float32)
    gain_f = gain.astype(jnp.float32)
    scale = lax.rsqrt(lax.optimization_barrier(jnp.mean(hidden_f * hidden_f, axis=-1, keepdims=True)) + epsilon)
    normed = (hidden_f * scale * gain_f).astype(jnp.bfloat16)
    keys = jnp.dot(normed, weight, preferred_element_type=jnp.float32).astype(jnp.bfloat16)
    back = jnp.dot(cotangent, weight.T, preferred_element_type=jnp.float32)
    upper = back * gain_f
    inner = lax.optimization_barrier(jnp.mean(upper * hidden_f, axis=-1, keepdims=True))
    grad_in = (scale * upper - hidden_f * scale * scale * scale * inner).astype(jnp.bfloat16)
    blocks_in = normed.reshape(N_FSDP, TOK_DEV, D)
    blocks_co = cotangent.reshape(N_FSDP, TOK_DEV, KC)

    def add_block(total, pair):
        term = jnp.dot(pair[0].T, pair[1], preferred_element_type=jnp.float32)
        return (total + term, None)
    grad_w, unused = lax.scan(add_block, jnp.zeros((D, KC), jnp.float32), (blocks_in, blocks_co))
    return (keys, grad_in, grad_w)

def reference(hidden_in, norm_gain, key_weight, key_cotangent, frag_global, frag_moment, frag_local):
    keys, grad_in, grad_w = lax.map(one_island, (hidden_in, norm_gain, key_weight, key_cotangent))
    pseudo = lax.optimization_barrier(jnp.sum(frag_global[None] - frag_local.astype(jnp.float32), axis=0)) / N_ISLAND
    new_moment = outer_momentum * frag_moment + pseudo
    new_global = frag_global - outer_rate * (pseudo + outer_momentum * new_moment)
    new_local = (mix_weight * frag_local.astype(jnp.float32) + (1.0 - mix_weight) * new_global[None]).astype(jnp.bfloat16)
    return (keys, grad_in, grad_w, new_global, new_moment, new_local)
```

```python
import jax
import jax.numpy as jnp
from jax import lax
from jax.experimental import pallas as pl
from jax.experimental.pallas import tpu as pltpu
from jax.sharding import PartitionSpec as P

epsilon = 1e-05
outer_rate = 0.7
outer_momentum = 0.9
mix_weight = 0.5

MESH = pl.DeviceIdType.MESH
F32 = jnp.float32
BF16 = jnp.bfloat16

D = 8192
KC = 512
TOK = 256
NZ = 8
ISLANDS = 8
NCHIP = 16
HALF = 128
SIGNS = (1, -1)


def norm_dz(dz):
    dz = dz % NZ
    return dz - NZ if dz > 4 else dz


def copy_names():
    names = []
    for d in (0, 1):
        for k in (1, 2, 3, 4):
            for dy in (0, 1):
                if k <= chain_len(d, dy):
                    names += [("gA", d, dy, k), ("rA", d, dy, k)]
            names += [("gB", d, k), ("rB", d, k)]
    names += [("gyA",), ("ryA",), ("own",), ("cot",), ("n", 0), ("n", 1)]
    for dz in range(-3, 5):
        names += [("gyB", dz), ("ryB", dz)]
        for dy in (0, 1):
            if (dy, dz) != (0, 0):
                names += [("sA", dy, dz), ("sB", dy, dz)]
    for j in (1, 2, 3):
        names += [("fx", j), ("ft", j)]
    names += [("fy",)]
    return {name: i for i, name in enumerate(names)}


def chain_len(d, dy):
    return 4 if d == dy else 3


NAMES = copy_names()


def kernel(
    hid_h, gain_h, w_h, cot_h, fg_h, fm_h, fl_h,
    keys_o, gi_o, gw_o, ng_o, nm_o, nl_o,
    w, hid, nrm, nsib, upper, part, gain, cot, cot_t, kacc, iacc, scl,
    fg, fm, fl, fx, fs, ftot,
    r_a, st_a, yb_s, yb_r, r_b, st_b, ya_s, ya_r,
    ssem, rsem, lsem,
):
    island = lax.axis_index("island")
    f = lax.axis_index("fsdp")
    c = lax.rem(f, 2)
    z = lax.rem(lax.div(f, 2), NZ)
    y = lax.div(f, 2 * NZ)
    x = lax.rem(island, 4)
    yh = lax.div(island, 4)

    def fsdp_of(yy, zz, cc):
        return (yy * NZ + zz) * 2 + cc

    def q_of(dy, dz):
        yy = y if dy == 0 else 1 - y
        return yy * NZ + lax.rem(z + (dz + NZ), NZ)

    zdev = [
        (island, fsdp_of(y, lax.rem(z + 1, NZ), c)),
        (island, fsdp_of(y, lax.rem(z + NZ - 1, NZ), c)),
    ]
    ydev = (island, fsdp_of(1 - y, z, c))
    sdev = (island, fsdp_of(y, z, 1 - c))
    xdev = {j: (yh * 4 + lax.rem(x + j, 4), f) for j in (1, 2, 3)}
    hdev = ((1 - yh) * 4 + x, f)
    peers = zdev + [ydev, sdev, hdev] + [xdev[j] for j in (1, 2, 3)]

    sent = []

    def send(name, src, dst, dev):
        i = NAMES[name]
        copy = pltpu.make_async_remote_copy(
            src_ref=src, dst_ref=dst, send_sem=ssem.at[i], recv_sem=rsem.at[i],
            device_id=dev, device_id_type=MESH,
        )
        copy.start()
        sent.append(copy)

    def arrive(name, dst, dev):
        i = NAMES[name]
        pltpu.make_async_remote_copy(
            src_ref=dst, dst_ref=dst, send_sem=ssem.at[i], recv_sem=rsem.at[i],
            device_id=dev, device_id_type=MESH,
        ).wait_recv()

    loads = [
        (w_h.at[0], w.at[pl.ds(pl.multiple_of((y * NZ + z) * 512 + c * 256, 256), 256)]),
        (cot_h.at[0], cot.at[0]),
        (fl_h.at[0], fl),
        (gain_h, gain),
        (hid_h.at[0, pl.ds(0, 128)], hid.at[pl.ds(0, 128)]),
        (hid_h.at[0, pl.ds(128, 128)], hid.at[pl.ds(128, 128)]),
        (fg_h, fg),
        (fm_h, fm),
    ]
    local = [pltpu.make_async_copy(s, t, lsem.at[i]) for i, (s, t) in enumerate(loads)]
    for copy in local:
        copy.start()

    barrier = pltpu.get_barrier_semaphore()
    for dev in peers:
        pl.semaphore_signal(barrier, inc=1, device_id=dev, device_id_type=MESH)
    pl.semaphore_wait(barrier, len(peers))

    def wrows(dy, dz, start, size, core=None):
        core = c if core is None else core
        row = q_of(dy, dz) * 512 + core * 256 + start
        return w.at[pl.ds(pl.multiple_of(row, 32), size)]

    def b_span(d, k):
        if k < 4:
            return HALF, 256 - HALF
        half = (256 - HALF) // 2
        return (HALF, half) if d == 0 else (HALF + half, half)

    def g_send_a(d, dy, k):
        part_ = wrows(dy, norm_dz(-SIGNS[d] * (k - 1)), 0, HALF)
        send(("gA", d, dy, k), part_, part_, zdev[d])

    def g_send_b(d, k):
        start, size = b_span(d, k)
        part_ = wrows(0, norm_dz(-SIGNS[d] * (k - 1)), start, size)
        send(("gB", d, k), part_, part_, zdev[d])

    def g_send_yb(dz):
        part_ = wrows(0, dz, HALF, 256 - HALF)
        send(("gyB", dz), part_, part_, ydev)

    def to_sibling(which, dy, dz):
        start, size = (0, HALF) if which == "sA" else (HALF, 256 - HALF)
        part_ = wrows(dy, dz, start, size)
        send((which, dy, dz), part_, part_, sdev)

    def from_sibling(dy, dz):
        if (dy, dz) == (0, 0):
            arrive(("own",), wrows(0, 0, 0, 256, 1 - c), sdev)
            return
        arrive(("sA", dy, dz), wrows(dy, dz, 0, HALF, 1 - c), sdev)
        arrive(("sB", dy, dz), wrows(dy, dz, HALF, 256 - HALF, 1 - c), sdev)

    def g_recv_a(dy, k):
        for d in (0, 1):
            if k <= chain_len(d, dy):
                dz = norm_dz(-SIGNS[d] * k)
                arrive(("gA", d, dy, k), wrows(dy, dz, 0, HALF), zdev[d])
                if k < chain_len(d, dy):
                    g_send_a(d, dy, k + 1)
                to_sibling("sA", dy, dz)

    def g_recv_b(k):
        for d in (0, 1):
            dz = norm_dz(-SIGNS[d] * k)
            start, size = b_span(d, k)
            arrive(("gB", d, k), wrows(0, dz, start, size), zdev[d])
            if k < 4:
                g_send_b(d, k + 1)
            if k < 4 or d == 1:
                g_send_yb(dz)
                to_sibling("sB", 0, dz)

    def g_recv_yb(dz):
        arrive(("gyB", dz), wrows(1, dz, HALF, 256 - HALF), ydev)
        to_sibling("sB", 1, dz)

    def norm_block(i, carry):
        rows = pl.ds(pl.multiple_of(i * 32, 32), 32)
        acc = jnp.zeros((32, 512), F32)
        for j in range(16):
            h = hid[rows, j * 512:(j + 1) * 512].astype(F32)
            acc = acc + h * h
        total = jnp.sum(acc, axis=-1, keepdims=True)
        s = lax.rsqrt(total / D + epsilon)
        scl[rows, :] = s
        for j in range(16):
            h = hid[rows, j * 512:(j + 1) * 512].astype(F32)
            g = gain[:, j * 512:(j + 1) * 512].astype(F32)
            n = (h * s * g).astype(BF16)
            nrm[0, rows, j * 256:(j + 1) * 256] = n[:, :256]
            nrm[1, rows, j * 256:(j + 1) * 256] = n[:, 256:]
        return carry

    def norm_half(i):
        lax.fori_loop(i * 4, i * 4 + 4, norm_block, 0)
        rows = pl.ds(i * 128, 128)
        send(("n", i), nrm.at[1 - c, rows], nsib.at[rows], sdev)

    def part_block(q, carry):
        cols = pl.ds(pl.multiple_of(q * 256, 256), 256)
        a = jnp.dot(cot_t[0], nrm[c, :, cols], preferred_element_type=F32)
        b = jnp.dot(cot_t[1], nsib[:, cols], preferred_element_type=F32)
        part[q] = a + b
        return carry

    def work_on(q):
        cols = pl.ds(pl.multiple_of(q * 512, 512), 512)
        half = pl.ds(pl.multiple_of(q * 256, 256), 256)
        rows = pl.multiple_of(q * 512, 512)
        w0 = w[pl.ds(rows, 256), :]
        w1 = w[pl.ds(rows + 256, 256), :]
        kacc[...] += jnp.dot(nrm[0, :, half], w0, preferred_element_type=F32) + jnp.dot(
            nrm[1, :, half], w1, preferred_element_type=F32
        )
        back = lax.dot_general(
            cot[0], w[pl.ds(rows, 512), :], (((1,), (1,)), ((), ())), preferred_element_type=F32
        )
        u = back * gain[:, cols].astype(F32)
        upper[:, cols] = u
        t = u * hid[:, cols].astype(F32)
        iacc[...] += (t[:, :128] + t[:, 128:256]) + (t[:, 256:384] + t[:, 384:])

    def work_round(d):
        if d == 0 or d == 4:
            for dy in (0, 1):
                from_sibling(dy, d)
            lax.fori_loop(0, 2, lambda i, carry: (work_on(lax.rem(y + i, 2) * NZ + lax.rem(z + d, NZ)), carry)[1], 0)
            return
        for dz in (d, -d):
            for dy in (0, 1):
                from_sibling(dy, dz)

        def one(i, carry):
            zz = lax.rem(z + NZ + d - 2 * d * lax.div(i, 2), NZ)
            work_on(lax.rem(y + lax.rem(i, 2), 2) * NZ + zz)
            return carry

        lax.fori_loop(0, 4, one, 0)

    def add_into(dst, terms, rows, step=64):
        def one(i, carry):
            r = pl.ds(pl.multiple_of(i * step, step), step)
            total = terms[0][r, :].astype(F32)
            for term in terms[1:]:
                total = total + term[r, :].astype(F32)
            dst[r, :] = total.astype(dst.dtype)
            return carry

        lax.fori_loop(0, rows // step, one, 0)

    def p_rows(dy, dz, start, size):
        return part.at[q_of(dy, dz), pl.ds(start, size)]

    def r_send_yb(dz):
        slot = dz + 3
        add_into(yb_s.at[slot], [p_rows(1, dz, 256, 256)], 256)
        send(("ryB", dz), yb_s.at[slot], yb_r.at[slot], ydev)

    def r_step_a(t, dy):
        for d in (0, 1):
            if t == 1 and chain_len(d, dy) == 3:
                continue
            dz = norm_dz(SIGNS[d] * (5 - t))
            mine = p_rows(dy, dz, 0, 256)
            if t == 1 or (t == 2 and chain_len(d, dy) == 3):
                buf = st_a.at[d, dy]
                add_into(buf, [mine], 256)
            else:
                buf = r_a.at[d, dy, t - 2]
                arrive(("rA", d, dy, r_index(d, dy, t - 1)), buf, zdev[d])
                add_into(buf, [buf, mine], 256)
            send(("rA", d, dy, r_index(d, dy, t)), buf, r_a.at[d, dy, t - 1], zdev[d])

    def r_index(d, dy, t):
        return t - (4 - chain_len(d, dy))

    def r_step_b(t):
        for d in (0, 1):
            dz = norm_dz(SIGNS[d] * (5 - t))
            slot = dz + 3
            if t == 1:
                if d == 0:
                    arrive(("ryB", dz), yb_r.at[slot], ydev)
                start = d * 128
                add_into(
                    st_b.at[d],
                    [p_rows(0, dz, 256 + start, 128), yb_r.at[slot, pl.ds(start, 128)]], 128,
                )
                send(("rB", d, 1), st_b.at[d], r_b.at[d, 0, pl.ds(start, 128)], zdev[d])
                continue
            arrive(("ryB", dz), yb_r.at[slot], ydev)
            buf = r_b.at[d, t - 2]
            if t == 2:
                start = d * 128
                other = 128 - start
                add_into(
                    buf.at[pl.ds(other, 128)],
                    [p_rows(0, dz, 256 + other, 128), yb_r.at[slot, pl.ds(other, 128)]], 128,
                )
                arrive(("rB", d, 1), buf.at[pl.ds(start, 128)], zdev[d])
                add_into(
                    buf.at[pl.ds(start, 128)],
                    [buf.at[pl.ds(start, 128)], p_rows(0, dz, 256 + start, 128), yb_r.at[slot, pl.ds(start, 128)]],
                    128,
                )
            else:
                arrive(("rB", d, t - 1), buf, zdev[d])
                add_into(buf, [buf, p_rows(0, dz, 256, 256), yb_r.at[slot]], 256)
            send(("rB", d, t), buf, r_b.at[d, t - 1], zdev[d])

    def r_last_a(dy):
        for d in (0, 1):
            arrive(("rA", d, dy, r_index(d, dy, 4)), r_a.at[d, dy, 3], zdev[d])
        return [p_rows(dy, 0, 0, 256), r_a.at[0, dy, 3], r_a.at[1, dy, 3]]

    def write_gw(start, terms):
        for i in range(2):
            r = slice(i * 128, (i + 1) * 128)
            total = terms[0][r, :].astype(F32)
            for term in terms[1:]:
                total = total + term[r, :].astype(F32)
            gw_o[0, :, start + i * 128:start + (i + 1) * 128] = total.T

    for i in range(3):
        local[i].wait()
    send(("gyA",), wrows(0, 0, 0, HALF), wrows(0, 0, 0, HALF), ydev)
    for d in (0, 1):
        g_send_a(d, 0, 1)
    for d in (0, 1):
        g_send_b(d, 1)
    g_send_yb(0)
    send(("own",), wrows(0, 0, 0, 256), wrows(0, 0, 0, 256), sdev)
    send(("cot",), cot.at[0], cot.at[1], sdev)
    for j in (1, 2, 3):
        quarter = pl.ds(pl.multiple_of(lax.rem(x + j, 4) * 64, 64), 64)
        send(("fx", j), fl.at[quarter], fx.at[j - 1], xdev[j])

    kacc[...] = jnp.zeros_like(kacc)
    iacc[...] = jnp.zeros_like(iacc)
    cot_t[0] = cot[0].T

    local[3].wait()
    local[4].wait()
    norm_half(0)
    arrive(("gyA",), wrows(1, 0, 0, HALF), ydev)
    for d in (0, 1):
        g_send_a(d, 1, 1)
    to_sibling("sA", 1, 0)
    local[5].wait()
    norm_half(1)
    g_recv_yb(0)
    g_recv_a(0, 1)
    g_recv_b(1)
    g_recv_a(1, 1)

    arrive(("cot",), cot.at[1], sdev)
    cot_t[1] = cot[1].T
    for i in (0, 1):
        arrive(("n", i), nsib.at[pl.ds(i * 128, 128)], sdev)
    lax.fori_loop(0, NCHIP, part_block, 0)
    for dz in (4, 3, -3):
        r_send_yb(dz)
    r_step_a(1, 1)
    r_step_a(1, 0)

    g_recv_a(0, 2)
    g_recv_b(2)
    g_recv_a(1, 2)
    for dz in (1, -1):
        g_recv_yb(dz)
    r_step_b(1)

    mine64 = pl.ds(pl.multiple_of(x * 64, 64), 64)
    total = fl[mine64, :].astype(F32)
    others = []
    for j in (1, 2, 3):
        arrive(("fx", j), fx.at[j - 1], xdev[j])
        others.append(fx[j - 1].astype(F32))
    fs[0] = (total + others[1]) + (others[0] + others[2])
    send(("fy",), fs.at[0], fs.at[1], hdev)

    work_round(0)

    g_recv_a(0, 3)
    g_recv_b(3)
    g_recv_a(1, 3)
    for dz in (2, -2):
        r_send_yb(dz)
        g_recv_yb(dz)
    r_step_a(2, 1)
    r_step_a(2, 0)
    r_step_b(2)

    work_round(1)

    arrive(("fy",), fs.at[1], hdev)
    ftot[mine64, :] = (fs[0] + fs[1]) / ISLANDS
    for j in (1, 2, 3):
        send(("ft", j), ftot.at[mine64], ftot.at[mine64], xdev[j])

    g_recv_a(0, 4)
    g_recv_b(4)
    g_recv_a(1, 4)
    for dz in (1, -1, 0):
        r_send_yb(dz)
    r_step_a(3, 1)
    r_step_a(3, 0)
    r_step_b(3)

    work_round(2)

    for j in (1, 2, 3):
        quarter = pl.ds(pl.multiple_of(lax.rem(x + 4 - j, 4) * 64, 64), 64)
        arrive(("ft", j), ftot.at[quarter], xdev[j])
    local[6].wait()
    local[7].wait()

    def outer(i, carry):
        r = pl.ds(pl.multiple_of(i * 32, 32), 32)
        g = fg[r, :]
        pseudo = g - ftot[r, :]
        moment = outer_momentum * fm[r, :] + pseudo
        new = g - outer_rate * (pseudo + outer_momentum * moment)
        nm_o[r, :] = moment
        ng_o[r, :] = new
        nl_o[0, r, :] = (mix_weight * fl[r, :].astype(F32) + (1.0 - mix_weight) * new).astype(BF16)
        return carry

    lax.fori_loop(0, 8, outer, 0)

    for dz in (3, -3, 4):
        g_recv_yb(dz)
    r_step_a(4, 1)
    r_step_a(4, 0)
    r_step_b(4)

    work_round(3)
    work_round(4)
    keys_o[0] = kacc[...].astype(BF16)

    def finish(i, carry):
        r = pl.ds(pl.multiple_of(i * 32, 32), 32)
        s = scl[r, :]
        inner = jnp.sum(iacc[r, :], axis=-1, keepdims=True) / D
        coef = s * s * s * inner
        for j in range(16):
            cols = slice(j * 512, (j + 1) * 512)
            gi_o[0, r, cols] = (s * upper[r, cols] - hid[r, cols].astype(F32) * coef).astype(BF16)
        return carry

    lax.fori_loop(0, 8, finish, 0)

    add_into(ya_s, r_last_a(1), 256)
    send(("ryA",), ya_s, ya_r, ydev)
    arrive(("ryB", 0), yb_r.at[3], ydev)
    for d in (0, 1):
        arrive(("rB", d, 4), r_b.at[d, 3], zdev[d])
    write_gw(256, [p_rows(0, 0, 256, 256), yb_r.at[3], r_b.at[0, 3], r_b.at[1, 3]])
    terms = r_last_a(0)
    arrive(("ryA",), ya_r, ydev)
    write_gw(0, terms + [ya_r])

    for copy in sent:
        copy.wait_send()


def store(*refs):
    n = (len(refs) - 1) // 2
    copies = [pltpu.make_async_copy(refs[i], refs[n + i], refs[-1].at[i]) for i in range(n)]
    for copy in copies:
        copy.start()
    for copy in copies:
        copy.wait()


def body(*args):
    outs = [
        ((1, TOK, KC), BF16),
        ((1, TOK, D), BF16),
        ((1, TOK, KC), F32),
        ((TOK, KC), F32),
        ((TOK, KC), F32),
        ((1, TOK, KC), BF16),
    ]
    vm = pltpu.VMEM
    results = pl.pallas_call(
        kernel,
        out_shape=[vm(*o) for o in outs],
        in_specs=[pl.BlockSpec(memory_space=pltpu.HBM)] * 7,
        out_specs=[pl.BlockSpec(memory_space=vm)] * 6,
        scratch_shapes=[
            vm((D, KC), BF16),
            vm((TOK, D), BF16),
            vm((2, TOK, D // 2), BF16),
            vm((TOK, D // 2), BF16),
            vm((TOK, D), F32),
            vm((NCHIP, KC, 256), F32),
            vm((1, D), BF16),
            vm((2, TOK, KC), BF16),
            vm((2, KC, TOK), BF16),
            vm((TOK, KC), F32),
            vm((TOK, 128), F32),
            vm((TOK, 1), F32),
            vm((TOK, KC), F32),
            vm((TOK, KC), F32),
            vm((TOK, KC), BF16),
            vm((3, 64, KC), BF16),
            vm((2, 64, KC), F32),
            vm((TOK, KC), F32),
            vm((2, 2, 4, 256, 256), BF16),
            vm((2, 2, 256, 256), BF16),
            vm((8, 256, 256), BF16),
            vm((8, 256, 256), BF16),
            vm((2, 4, 256, 256), BF16),
            vm((2, 128, 256), BF16),
            vm((256, 256), BF16),
            vm((256, 256), BF16),
            pltpu.SemaphoreType.DMA((len(NAMES),)),
            pltpu.SemaphoreType.DMA((len(NAMES),)),
            pltpu.SemaphoreType.DMA((8,)),
        ],
        compiler_params=pltpu.CompilerParams(
            collective_id=0, has_side_effects=True, vmem_limit_bytes=56 * 2**20
        ),
    )(*args)
    return tuple(
        pl.pallas_call(
            store,
            out_shape=[jax.ShapeDtypeStruct(*o) for o in outs],
            in_specs=[pl.BlockSpec(memory_space=vm)] * 6,
            out_specs=[pl.BlockSpec(memory_space=pl.ANY)] * 6,
            scratch_shapes=[pltpu.SemaphoreType.DMA((6,))],
        )(*results)
    )


def solution(mesh):
    rows = P("island", "fsdp", None)
    frag = P("fsdp", None)
    return jax.shard_map(
        body,
        mesh=mesh,
        in_specs=(rows, P("island", None), rows, rows, frag, frag, rows),
        out_specs=(rows, rows, rows, frag, frag, rows),
        check_vma=False,
    )
```

```python
import jax
import jax.numpy as jnp
from jax import lax
from jax.experimental import pallas as pl
from jax.experimental.pallas import tpu as pltpu
from jax.sharding import PartitionSpec as P

epsilon = 1e-05
outer_rate = 0.7
outer_momentum = 0.9
mix_weight = 0.5

MESH = pl.DeviceIdType.MESH
F32 = jnp.float32
BF16 = jnp.bfloat16

D = 8192
KC = 512
TOK = 256
NZ = 8
ISLANDS = 8
NCHIP = 16
HALF = 128
SIGNS = (1, -1)


def norm_dz(dz):
    dz = dz % NZ
    return dz - NZ if dz > 4 else dz


def copy_names():
    names = []
    for d in (0, 1):
        for k in (1, 2, 3, 4):
            for dy in (0, 1):
                if k <= chain_len(d, dy):
                    names += [("gA", d, dy, k), ("rA", d, dy, k)]
            names += [("gB", d, k), ("rB", d, k)]
    names += [("gyA",), ("ryA",), ("own",), ("cot",), ("n", 0), ("n", 1)]
    for dz in range(-3, 5):
        names += [("gyB", dz), ("ryB", dz)]
        for dy in (0, 1):
            if (dy, dz) != (0, 0):
                names += [("sA", dy, dz), ("sB", dy, dz)]
    for j in (1, 2, 3):
        names += [("fx", j), ("ft", j)]
    names += [("fy",)]
    return {name: i for i, name in enumerate(names)}


def chain_len(d, dy):
    return 4 if d == dy else 3


NAMES = copy_names()


def kernel(
    hid_h, gain_h, w_h, cot_h, fg_h, fm_h, fl_h,
    keys_o, gi_o, gw_o, ng_o, nm_o, nl_o,
    w, hid, nrm, nsib, upper, part, gain, cot, cot_t, kacc, iacc, scl,
    fg, fm, fl, fx, fs, ftot,
    r_a, st_a, yb_s, yb_r, r_b, st_b, ya_s, ya_r,
    ssem, rsem, lsem,
):
    island = lax.axis_index("island")
    f = lax.axis_index("fsdp")
    c = lax.rem(f, 2)
    z = lax.rem(lax.div(f, 2), NZ)
    y = lax.div(f, 2 * NZ)
    x = lax.rem(island, 4)
    yh = lax.div(island, 4)

    def fsdp_of(yy, zz, cc):
        return (yy * NZ + zz) * 2 + cc

    def q_of(dy, dz):
        yy = y if dy == 0 else 1 - y
        return yy * NZ + lax.rem(z + (dz + NZ), NZ)

    zdev = [
        (island, fsdp_of(y, lax.rem(z + 1, NZ), c)),
        (island, fsdp_of(y, lax.rem(z + NZ - 1, NZ), c)),
    ]
    ydev = (island, fsdp_of(1 - y, z, c))
    sdev = (island, fsdp_of(y, z, 1 - c))
    xdev = {j: (yh * 4 + lax.rem(x + j, 4), f) for j in (1, 2, 3)}
    hdev = ((1 - yh) * 4 + x, f)
    peers = zdev + [ydev, sdev, hdev] + [xdev[j] for j in (1, 2, 3)]

    sent = []

    def send(name, src, dst, dev):
        i = NAMES[name]
        copy = pltpu.make_async_remote_copy(
            src_ref=src, dst_ref=dst, send_sem=ssem.at[i], recv_sem=rsem.at[i],
            device_id=dev, device_id_type=MESH,
        )
        copy.start()
        sent.append(copy)

    def arrive(name, dst, dev):
        i = NAMES[name]
        pltpu.make_async_remote_copy(
            src_ref=dst, dst_ref=dst, send_sem=ssem.at[i], recv_sem=rsem.at[i],
            device_id=dev, device_id_type=MESH,
        ).wait_recv()

    loads = [
        (w_h.at[0], w.at[pl.ds(pl.multiple_of((y * NZ + z) * 512 + c * 256, 256), 256)]),
        (cot_h.at[0], cot.at[0]),
        (fl_h.at[0], fl),
        (gain_h, gain),
        (hid_h.at[0, pl.ds(0, 128)], hid.at[pl.ds(0, 128)]),
        (hid_h.at[0, pl.ds(128, 128)], hid.at[pl.ds(128, 128)]),
        (fg_h, fg),
        (fm_h, fm),
    ]
    local = [pltpu.make_async_copy(s, t, lsem.at[i]) for i, (s, t) in enumerate(loads)]
    for copy in local:
        copy.start()

    barrier = pltpu.get_barrier_semaphore()
    for dev in peers:
        pl.semaphore_signal(barrier, inc=1, device_id=dev, device_id_type=MESH)
    pl.semaphore_wait(barrier, len(peers))

    def wrows(dy, dz, start, size, core=None):
        core = c if core is None else core
        row = q_of(dy, dz) * 512 + core * 256 + start
        return w.at[pl.ds(pl.multiple_of(row, 32), size)]

    def b_span(d, k):
        if k < 4:
            return HALF, 256 - HALF
        half = (256 - HALF) // 2
        return (HALF, half) if d == 0 else (HALF + half, half)

    def g_send_a(d, dy, k):
        part_ = wrows(dy, norm_dz(-SIGNS[d] * (k - 1)), 0, HALF)
        send(("gA", d, dy, k), part_, part_, zdev[d])

    def g_send_b(d, k):
        start, size = b_span(d, k)
        part_ = wrows(0, norm_dz(-SIGNS[d] * (k - 1)), start, size)
        send(("gB", d, k), part_, part_, zdev[d])

    def g_send_yb(dz):
        part_ = wrows(0, dz, HALF, 256 - HALF)
        send(("gyB", dz), part_, part_, ydev)

    def to_sibling(which, dy, dz):
        start, size = (0, HALF) if which == "sA" else (HALF, 256 - HALF)
        part_ = wrows(dy, dz, start, size)
        send((which, dy, dz), part_, part_, sdev)

    def from_sibling(dy, dz):
        if (dy, dz) == (0, 0):
            arrive(("own",), wrows(0, 0, 0, 256, 1 - c), sdev)
            return
        arrive(("sA", dy, dz), wrows(dy, dz, 0, HALF, 1 - c), sdev)
        arrive(("sB", dy, dz), wrows(dy, dz, HALF, 256 - HALF, 1 - c), sdev)

    def g_recv_a(dy, k):
        for d in (0, 1):
            if k <= chain_len(d, dy):
                dz = norm_dz(-SIGNS[d] * k)
                arrive(("gA", d, dy, k), wrows(dy, dz, 0, HALF), zdev[d])
                if k < chain_len(d, dy):
                    g_send_a(d, dy, k + 1)
                to_sibling("sA", dy, dz)

    def g_recv_b(k):
        for d in (0, 1):
            dz = norm_dz(-SIGNS[d] * k)
            start, size = b_span(d, k)
            arrive(("gB", d, k), wrows(0, dz, start, size), zdev[d])
            if k < 4:
                g_send_b(d, k + 1)
            if k < 4 or d == 1:
                g_send_yb(dz)
                to_sibling("sB", 0, dz)

    def g_recv_yb(dz):
        arrive(("gyB", dz), wrows(1, dz, HALF, 256 - HALF), ydev)
        to_sibling("sB", 1, dz)

    def norm_block(i, carry):
        rows = pl.ds(pl.multiple_of(i * 32, 32), 32)
        acc = jnp.zeros((32, 512), F32)
        for j in range(16):
            h = hid[rows, j * 512:(j + 1) * 512].astype(F32)
            acc = acc + h * h
        total = jnp.sum(acc, axis=-1, keepdims=True)
        s = lax.rsqrt(total / D + epsilon)
        scl[rows, :] = s
        for j in range(16):
            h = hid[rows, j * 512:(j + 1) * 512].astype(F32)
            g = gain[:, j * 512:(j + 1) * 512].astype(F32)
            n = (h * s * g).astype(BF16)
            nrm[0, rows, j * 256:(j + 1) * 256] = n[:, :256]
            nrm[1, rows, j * 256:(j + 1) * 256] = n[:, 256:]
        return carry

    def norm_half(i):
        lax.fori_loop(i * 4, i * 4 + 4, norm_block, 0)
        rows = pl.ds(i * 128, 128)
        send(("n", i), nrm.at[1 - c, rows], nsib.at[rows], sdev)

    def part_block(q, carry):
        cols = pl.ds(pl.multiple_of(q * 256, 256), 256)
        a = jnp.dot(cot_t[0], nrm[c, :, cols], preferred_element_type=F32)
        b = jnp.dot(cot_t[1], nsib[:, cols], preferred_element_type=F32)
        part[q] = a + b
        return carry

    def work_on(q):
        cols = pl.ds(pl.multiple_of(q * 512, 512), 512)
        half = pl.ds(pl.multiple_of(q * 256, 256), 256)
        rows = pl.multiple_of(q * 512, 512)
        w0 = w[pl.ds(rows, 256), :]
        w1 = w[pl.ds(rows + 256, 256), :]
        kacc[...] += jnp.dot(nrm[0, :, half], w0, preferred_element_type=F32) + jnp.dot(
            nrm[1, :, half], w1, preferred_element_type=F32
        )
        back = lax.dot_general(
            cot[0], w[pl.ds(rows, 512), :], (((1,), (1,)), ((), ())), preferred_element_type=F32
        )
        u = back * gain[:, cols].astype(F32)
        upper[:, cols] = u
        t = u * hid[:, cols].astype(F32)
        iacc[...] += (t[:, :128] + t[:, 128:256]) + (t[:, 256:384] + t[:, 384:])

    def work_round(d):
        if d == 0 or d == 4:
            for dy in (0, 1):
                from_sibling(dy, d)
            lax.fori_loop(0, 2, lambda i, carry: (work_on(lax.rem(y + i, 2) * NZ + lax.rem(z + d, NZ)), carry)[1], 0)
            return
        for dz in (d, -d):
            for dy in (0, 1):
                from_sibling(dy, dz)

        def one(i, carry):
            zz = lax.rem(z + NZ + d - 2 * d * lax.div(i, 2), NZ)
            work_on(lax.rem(y + lax.rem(i, 2), 2) * NZ + zz)
            return carry

        lax.fori_loop(0, 4, one, 0)

    def add_into(dst, terms, rows, step=64):
        def one(i, carry):
            r = pl.ds(pl.multiple_of(i * step, step), step)
            total = terms[0][r, :].astype(F32)
            for term in terms[1:]:
                total = total + term[r, :].astype(F32)
            dst[r, :] = total.astype(dst.dtype)
            return carry

        lax.fori_loop(0, rows // step, one, 0)

    def p_rows(dy, dz, start, size):
        return part.at[q_of(dy, dz), pl.ds(start, size)]

    def r_send_yb(dz):
        slot = dz + 3
        add_into(yb_s.at[slot], [p_rows(1, dz, 256, 256)], 256)
        send(("ryB", dz), yb_s.at[slot], yb_r.at[slot], ydev)

    def r_step_a(t, dy):
        for d in (0, 1):
            if t == 1 and chain_len(d, dy) == 3:
                continue
            dz = norm_dz(SIGNS[d] * (5 - t))
            mine = p_rows(dy, dz, 0, 256)
            if t == 1 or (t == 2 and chain_len(d, dy) == 3):
                buf = st_a.at[d, dy]
                add_into(buf, [mine], 256)
            else:
                buf = r_a.at[d, dy, t - 2]
                arrive(("rA", d, dy, r_index(d, dy, t - 1)), buf, zdev[d])
                add_into(buf, [buf, mine], 256)
            send(("rA", d, dy, r_index(d, dy, t)), buf, r_a.at[d, dy, t - 1], zdev[d])

    def r_index(d, dy, t):
        return t - (4 - chain_len(d, dy))

    def r_step_b(t):
        for d in (0, 1):
            dz = norm_dz(SIGNS[d] * (5 - t))
            slot = dz + 3
            if t == 1:
                if d == 0:
                    arrive(("ryB", dz), yb_r.at[slot], ydev)
                start = d * 128
                add_into(
                    st_b.at[d],
                    [p_rows(0, dz, 256 + start, 128), yb_r.at[slot, pl.ds(start, 128)]], 128,
                )
                send(("rB", d, 1), st_b.at[d], r_b.at[d, 0, pl.ds(start, 128)], zdev[d])
                continue
            arrive(("ryB", dz), yb_r.at[slot], ydev)
            buf = r_b.at[d, t - 2]
            if t == 2:
                start = d * 128
                other = 128 - start
                add_into(
                    buf.at[pl.ds(other, 128)],
                    [p_rows(0, dz, 256 + other, 128), yb_r.at[slot, pl.ds(other, 128)]], 128,
                )
                arrive(("rB", d, 1), buf.at[pl.ds(start, 128)], zdev[d])
                add_into(
                    buf.at[pl.ds(start, 128)],
                    [buf.at[pl.ds(start, 128)], p_rows(0, dz, 256 + start, 128), yb_r.at[slot, pl.ds(start, 128)]],
                    128,
                )
            else:
                arrive(("rB", d, t - 1), buf, zdev[d])
                add_into(buf, [buf, p_rows(0, dz, 256, 256), yb_r.at[slot]], 256)
            send(("rB", d, t), buf, r_b.at[d, t - 1], zdev[d])

    def r_last_a(dy):
        for d in (0, 1):
            arrive(("rA", d, dy, r_index(d, dy, 4)), r_a.at[d, dy, 3], zdev[d])
        return [p_rows(dy, 0, 0, 256), r_a.at[0, dy, 3], r_a.at[1, dy, 3]]

    def write_gw(start, terms):
        for i in range(2):
            r = slice(i * 128, (i + 1) * 128)
            total = terms[0][r, :].astype(F32)
            for term in terms[1:]:
                total = total + term[r, :].astype(F32)
            gw_o[0, :, start + i * 128:start + (i + 1) * 128] = total.T

    for i in range(3):
        local[i].wait()
    send(("gyA",), wrows(0, 0, 0, HALF), wrows(0, 0, 0, HALF), ydev)
    for d in (0, 1):
        g_send_a(d, 0, 1)
    for d in (0, 1):
        g_send_b(d, 1)
    g_send_yb(0)
    send(("own",), wrows(0, 0, 0, 256), wrows(0, 0, 0, 256), sdev)
    send(("cot",), cot.at[0], cot.at[1], sdev)
    for j in (1, 2, 3):
        quarter = pl.ds(pl.multiple_of(lax.rem(x + j, 4) * 64, 64), 64)
        send(("fx", j), fl.at[quarter], fx.at[j - 1], xdev[j])

    kacc[...] = jnp.zeros_like(kacc)
    iacc[...] = jnp.zeros_like(iacc)
    cot_t[0] = cot[0].T

    local[3].wait()
    local[4].wait()
    norm_half(0)
    arrive(("gyA",), wrows(1, 0, 0, HALF), ydev)
    for d in (0, 1):
        g_send_a(d, 1, 1)
    to_sibling("sA", 1, 0)
    local[5].wait()
    norm_half(1)
    g_recv_yb(0)
    g_recv_a(0, 1)
    g_recv_b(1)
    g_recv_a(1, 1)

    arrive(("cot",), cot.at[1], sdev)
    cot_t[1] = cot[1].T
    for i in (0, 1):
        arrive(("n", i), nsib.at[pl.ds(i * 128, 128)], sdev)
    lax.fori_loop(0, NCHIP, part_block, 0)
    for dz in (4, 3, -3):
        r_send_yb(dz)
    r_step_a(1, 1)
    r_step_a(1, 0)

    g_recv_a(0, 2)
    g_recv_b(2)
    g_recv_a(1, 2)
    for dz in (1, -1):
        g_recv_yb(dz)
    r_step_b(1)

    mine64 = pl.ds(pl.multiple_of(x * 64, 64), 64)
    total = fl[mine64, :].astype(F32)
    others = []
    for j in (1, 2, 3):
        arrive(("fx", j), fx.at[j - 1], xdev[j])
        others.append(fx[j - 1].astype(F32))
    fs[0] = (total + others[1]) + (others[0] + others[2])
    send(("fy",), fs.at[0], fs.at[1], hdev)

    work_round(0)

    g_recv_a(0, 3)
    g_recv_b(3)
    g_recv_a(1, 3)
    for dz in (2, -2):
        r_send_yb(dz)
        g_recv_yb(dz)
    r_step_a(2, 1)
    r_step_a(2, 0)
    r_step_b(2)

    work_round(1)

    arrive(("fy",), fs.at[1], hdev)
    ftot[mine64, :] = (fs[0] + fs[1]) / ISLANDS
    for j in (1, 2, 3):
        send(("ft", j), ftot.at[mine64], ftot.at[mine64], xdev[j])

    g_recv_a(0, 4)
    g_recv_b(4)
    g_recv_a(1, 4)
    for dz in (1, -1, 0):
        r_send_yb(dz)
    r_step_a(3, 1)
    r_step_a(3, 0)
    r_step_b(3)

    work_round(2)

    for j in (1, 2, 3):
        quarter = pl.ds(pl.multiple_of(lax.rem(x + 4 - j, 4) * 64, 64), 64)
        arrive(("ft", j), ftot.at[quarter], xdev[j])
    local[6].wait()
    local[7].wait()

    def outer(i, carry):
        r = pl.ds(pl.multiple_of(i * 32, 32), 32)
        g = fg[r, :]
        pseudo = g - ftot[r, :]
        moment = outer_momentum * fm[r, :] + pseudo
        new = g - outer_rate * (pseudo + outer_momentum * moment)
        nm_o[r, :] = moment
        ng_o[r, :] = new
        nl_o[0, r, :] = (mix_weight * fl[r, :].astype(F32) + (1.0 - mix_weight) * new).astype(BF16)
        return carry

    lax.fori_loop(0, 8, outer, 0)

    for dz in (3, -3, 4):
        g_recv_yb(dz)
    r_step_a(4, 1)
    r_step_a(4, 0)
    r_step_b(4)

    work_round(3)
    work_round(4)
    keys_o[0] = kacc[...].astype(BF16)

    def finish(i, carry):
        r = pl.ds(pl.multiple_of(i * 32, 32), 32)
        s = scl[r, :]
        inner = jnp.sum(iacc[r, :], axis=-1, keepdims=True) / D
        coef = s * s * s * inner
        for j in range(16):
            cols = slice(j * 512, (j + 1) * 512)
            gi_o[0, r, cols] = (s * upper[r, cols] - hid[r, cols].astype(F32) * coef).astype(BF16)
        return carry

    lax.fori_loop(0, 8, finish, 0)

    add_into(ya_s, r_last_a(1), 256)
    send(("ryA",), ya_s, ya_r, ydev)
    arrive(("ryB", 0), yb_r.at[3], ydev)
    for d in (0, 1):
        arrive(("rB", d, 4), r_b.at[d, 3], zdev[d])
    write_gw(256, [p_rows(0, 0, 256, 256), yb_r.at[3], r_b.at[0, 3], r_b.at[1, 3]])
    terms = r_last_a(0)
    arrive(("ryA",), ya_r, ydev)
    write_gw(0, terms + [ya_r])

    for copy in sent:
        copy.wait_send()


def store(*refs):
    n = (len(refs) - 1) // 2
    copies = [pltpu.make_async_copy(refs[i], refs[n + i], refs[-1].at[i]) for i in range(n)]
    for copy in copies:
        copy.start()
    for copy in copies:
        copy.wait()


def body(*args):
    outs = [
        ((1, TOK, KC), BF16),
        ((1, TOK, D), BF16),
        ((1, TOK, KC), F32),
        ((TOK, KC), F32),
        ((TOK, KC), F32),
        ((1, TOK, KC), BF16),
    ]
    vm = pltpu.VMEM
    results = pl.pallas_call(
        kernel,
        out_shape=[vm(*o) for o in outs],
        in_specs=[pl.BlockSpec(memory_space=pltpu.HBM)] * 7,
        out_specs=[pl.BlockSpec(memory_space=vm)] * 6,
        scratch_shapes=[
            vm((D, KC), BF16),
            vm((TOK, D), BF16),
            vm((2, TOK, D // 2), BF16),
            vm((TOK, D // 2), BF16),
            vm((TOK, D), F32),
            vm((NCHIP, KC, 256), F32),
            vm((1, D), BF16),
            vm((2, TOK, KC), BF16),
            vm((2, KC, TOK), BF16),
            vm((TOK, KC), F32),
            vm((TOK, 128), F32),
            vm((TOK, 1), F32),
            vm((TOK, KC), F32),
            vm((TOK, KC), F32),
            vm((TOK, KC), BF16),
            vm((3, 64, KC), BF16),
            vm((2, 64, KC), F32),
            vm((TOK, KC), F32),
            vm((2, 2, 4, 256, 256), BF16),
            vm((2, 2, 256, 256), BF16),
            vm((8, 256, 256), BF16),
            vm((8, 256, 256), BF16),
            vm((2, 4, 256, 256), BF16),
            vm((2, 128, 256), BF16),
            vm((256, 256), BF16),
            vm((256, 256), BF16),
            pltpu.SemaphoreType.DMA((len(NAMES),)),
            pltpu.SemaphoreType.DMA((len(NAMES),)),
            pltpu.SemaphoreType.DMA((8,)),
        ],
        compiler_params=pltpu.CompilerParams(
            collective_id=0, has_side_effects=True, vmem_limit_bytes=56 * 2**20
        ),
    )(*args)
    return tuple(
        pl.pallas_call(
            store,
            out_shape=[jax.ShapeDtypeStruct(*o) for o in outs],
            in_specs=[pl.BlockSpec(memory_space=pl.ANY)] * 6,
            out_specs=[pl.BlockSpec(memory_space=pl.ANY)] * 6,
            scratch_shapes=[pltpu.SemaphoreType.DMA((6,))],
            compiler_params=pltpu.CompilerParams(vmem_limit_bytes=2**20),
        )(*results)
    )


def solution(mesh):
    rows = P("island", "fsdp", None)
    frag = P("fsdp", None)
    return jax.shard_map(
        body,
        mesh=mesh,
        in_specs=(rows, P("island", None), rows, rows, frag, frag, rows),
        out_specs=(rows, rows, rows, frag, frag, rows),
        check_vma=False,
    )
```

```python
import math

import jax
import jax.numpy as jnp
from jax import lax
from jax.experimental import pallas as pl
from jax.experimental.pallas import tpu as pltpu
from jax.sharding import PartitionSpec as P

epsilon = 1e-05
outer_rate = 0.7
outer_momentum = 0.9
mix_weight = 0.5

MESH = pl.DeviceIdType.MESH
F32 = jnp.float32
BF16 = jnp.bfloat16

D = 8192
KC = 512
TOK = 256
NZ = 8
ISLANDS = 8
NCHIP = 16
HALF = 112
SIGNS = (1, -1)


def norm_dz(dz):
    dz = dz % NZ
    return dz - NZ if dz > 4 else dz


def chain_len(d, dy):
    return 4 if d == dy else 3


def arrival(name):
    kind = name[0]
    if kind in ("own", "sA", "sB"):
        return ("s", name[2] if len(name) > 1 else 0)
    if kind in ("cot", "n"):
        return ("n",)
    if kind in ("fx", "ft"):
        return (kind,)
    if kind in ("gB", "rB") and name[2] == 4:
        return (kind, 4)
    if kind == "rA" and name[3] == 4:
        return (kind, 4, name[2])
    return name


def arrivals():
    names = [("gyA",), ("ryA",), ("n",), ("fx",), ("fy",), ("fz",), ("ft",), ("gB", 4), ("rB", 4)]
    for dy in (0, 1):
        names += [("rA", 4, dy)]
        for d in (0, 1):
            names += [("gA", d, dy, k) for k in range(1, 1 + chain_len(d, dy))]
            names += [("rA", d, dy, t) for t in range(5 - chain_len(d, dy), 4)]
    for k in (1, 2, 3):
        names += [(kind, d, k) for kind in ("gB", "rB") for d in (0, 1)]
    for dz in range(-3, 5):
        names += [(kind, dz) for kind in ("gyB", "ryB", "s")]
    return {name: i for i, name in enumerate(names)}


ARRIVALS = arrivals()

ORDER = (
    ("start",), ("norm", 0), ("norm", 1), ("gB", 0, 1), ("gyA",), ("gB", 1, 1), ("gB", 0, 2), ("gA", 1, 1, 1),
    ("part", 0), ("ryB", 4), ("rA", 0, 1, 2), ("rA", 0, 0, 1), ("gB", 1, 2), ("rA", 1, 1, 1), ("gA", 1, 0, 1),
    ("gyB", -1), ("part", 1), ("rA", 0, 1, 3), ("gA", 0, 1, 1), ("rA", 1, 0, 2), ("rB", 1, 1), ("gA", 0, 0, 1),
    ("fx",), ("gB", 1, 3), ("part", 2), ("gyB", 2), ("rA", 1, 1, 2), ("ryB", -3), ("gA", 1, 0, 2), ("rA", 0, 0, 2),
    ("gyB", 1), ("ryB", 3), ("gA", 1, 1, 2), ("gB", 0, 3), ("part", 3), ("ryB", -2), ("gyB", -2), ("rA", 1, 0, 3),
    ("gA", 0, 1, 2), ("pair", -1), ("fy",), ("pair", 1), ("gB", 1, 4), ("rB", 0, 1), ("gA", 0, 0, 2), ("rA", 1, 1, 3),
    ("gyB", 0), ("fz",), ("gA", 1, 1, 3), ("gA", 1, 0, 3), ("rB", 0, 2), ("gA", 0, 0, 3), ("rB", 1, 2), ("ryB", 2),
    ("rA", 0, 0, 3), ("gA", 0, 1, 3), ("gyB", 3), ("gyB", -3), ("pair", 2), ("rA", 1, 1, 4), ("rA", 0, 1, 4),
    ("ryB", 1), ("ft",), ("gyB", 4), ("pair", 0), ("ryB", -1), ("pair", -2), ("rB", 1, 3), ("gA", 1, 1, 4),
    ("gA", 0, 0, 4), ("rB", 0, 3), ("pair", 3), ("rA", 1, 0, 4), ("rA", 0, 0, 4), ("ryB", 0), ("pair", -3),
    ("pair", 4), ("fin", 0), ("rB", 1, 4), ("ryA",), ("rB", 0, 4), ("fin", 1), ("fin", 2), ("fin", 3), ("endA",),
    ("endB",),
)

GROUPS = ((4, 3), (-3, 2), (-2, 1), (-1, 0))


def kernel(
    hid_h, gain_h, w_h, cot_h, fg_h, fm_h, fl_h,
    keys_o, gi_o, gw_o, ng_o, nm_o, nl_o,
    w, hid, nrm, nsib, upper, part, gain, cot, cot_t, kacc, iacc, scl,
    fg, fm, fl, fx, fs, ftot,
    r_a, st_a, yb_s, yb_r, r_b, st_b, ya_s, ya_r,
    ssem, rsem, lsem,
):
    island = lax.axis_index("island")
    f = lax.axis_index("fsdp")
    c = lax.rem(f, 2)
    z = lax.rem(lax.div(f, 2), NZ)
    y = lax.div(f, 2 * NZ)
    x = lax.rem(island, 4)
    yh = lax.div(island, 4)

    def fsdp_of(yy, zz, cc):
        return (yy * NZ + zz) * 2 + cc

    def q_of(dy, dz):
        yy = y if dy == 0 else 1 - y
        return yy * NZ + lax.rem(z + (dz + NZ), NZ)

    zdev = [
        (island, fsdp_of(y, lax.rem(z + 1, NZ), c)),
        (island, fsdp_of(y, lax.rem(z + NZ - 1, NZ), c)),
    ]
    ydev = (island, fsdp_of(1 - y, z, c))
    sdev = (island, fsdp_of(y, z, 1 - c))
    xdev = {j: (yh * 4 + lax.rem(x + j, 4), f) for j in (1, 2, 3)}
    hdev = ((1 - yh) * 4 + x, fsdp_of(1 - y, z, c))
    peers = zdev + [ydev, sdev, hdev] + [xdev[j] for j in (1, 2, 3)]

    sent = [0, 0]

    def send(name, src, dst, dev):
        group = 0 if name[0] in ("own", "gA", "gB", "gyA", "gyB", "sA", "sB") else 1
        pltpu.make_async_remote_copy(
            src_ref=src, dst_ref=dst, send_sem=ssem.at[group], recv_sem=rsem.at[ARRIVALS[arrival(name)]],
            device_id=dev, device_id_type=MESH,
        ).start()
        sent[group] += math.prod(src.shape) * src.dtype.itemsize

    def arrive(name, ref, dev):
        pltpu.make_async_remote_copy(
            src_ref=ref, dst_ref=ref, send_sem=ssem.at[0], recv_sem=rsem.at[ARRIVALS[name]],
            device_id=dev, device_id_type=MESH,
        ).wait_recv()

    loads = [
        (w_h.at[0], w.at[pl.ds(pl.multiple_of((y * NZ + z) * 512 + c * 256, 256), 256)]),
        (cot_h.at[0], cot.at[0]),
        (fl_h.at[0], fl),
        (gain_h, gain),
        (hid_h.at[0, pl.ds(0, 128)], hid.at[pl.ds(0, 128)]),
        (hid_h.at[0, pl.ds(128, 128)], hid.at[pl.ds(128, 128)]),
        (fg_h, fg),
        (fm_h, fm),
    ]
    local = [pltpu.make_async_copy(s, t, lsem.at[i]) for i, (s, t) in enumerate(loads)]
    for copy in local:
        copy.start()

    barrier = pltpu.get_barrier_semaphore()
    for dev in peers:
        pl.semaphore_signal(barrier, inc=1, device_id=dev, device_id_type=MESH)
    pl.semaphore_wait(barrier, len(peers))

    def wrows(dy, dz, start, size, core=None):
        core = c if core is None else core
        row = q_of(dy, dz) * 512 + core * 256 + start
        return w.at[pl.ds(pl.multiple_of(row, 16), size)]

    def b_span(d, k):
        if k < 4:
            return HALF, 256 - HALF
        half = (256 - HALF) // 32 * 16
        first = 256 - HALF - half
        return (HALF, first) if d == 0 else (HALF + first, half)

    def g_send_a(d, dy, k):
        part_ = wrows(dy, norm_dz(-SIGNS[d] * (k - 1)), 0, HALF)
        send(("gA", d, dy, k), part_, part_, zdev[d])

    def g_send_b(d, k):
        start, size = b_span(d, k)
        part_ = wrows(0, norm_dz(-SIGNS[d] * (k - 1)), start, size)
        send(("gB", d, k), part_, part_, zdev[d])

    def g_send_yb(dz):
        part_ = wrows(0, dz, HALF, 256 - HALF)
        send(("gyB", dz), part_, part_, ydev)

    def to_sibling(which, dy, dz):
        start, size = (0, HALF) if which == "sA" else (HALF, 256 - HALF)
        part_ = wrows(dy, dz, start, size)
        send((which, dy, dz), part_, part_, sdev)

    def step_start():
        for i in range(2):
            local[i].wait()
        send(("gyA",), wrows(0, 0, 0, HALF), wrows(0, 0, 0, HALF), ydev)
        for d in (0, 1):
            g_send_b(d, 1)
        g_send_yb(0)
        for d in (0, 1):
            g_send_a(d, 0, 1)
        send(("own",), wrows(0, 0, 0, 256), wrows(0, 0, 0, 256), sdev)
        send(("cot",), cot.at[0], cot.at[1], sdev)
        local[2].wait()
        for j in (1, 2, 3):
            quarter = pl.ds(pl.multiple_of(lax.rem(x + j, 4) * 64, 64), 64)
            send(("fx", j), fl.at[quarter], fx.at[j - 1], xdev[j])
        kacc[...] = jnp.zeros_like(kacc)
        iacc[...] = jnp.zeros_like(iacc)
        cot_t[0] = cot[0].T

    def step_gya():
        arrive(("gyA",), wrows(1, 0, 0, HALF), ydev)
        for d in (0, 1):
            g_send_a(d, 1, 1)
        to_sibling("sA", 1, 0)

    def step_ga(d, dy, k):
        dz = norm_dz(-SIGNS[d] * k)
        arrive(("gA", d, dy, k), wrows(dy, dz, 0, HALF), zdev[d])
        if k < chain_len(d, dy):
            g_send_a(d, dy, k + 1)
        to_sibling("sA", dy, dz)

    def step_gb(d, k):
        dz = norm_dz(-SIGNS[d] * k)
        if k == 4:
            arrive(("gB", 4), wrows(0, dz, HALF, 256 - HALF), zdev[d])
        else:
            arrive(("gB", d, k), wrows(0, dz, HALF, 256 - HALF), zdev[d])
            g_send_b(d, k + 1)
        g_send_yb(dz)
        to_sibling("sB", 0, dz)

    def step_gyb(dz):
        arrive(("gyB", dz), wrows(1, dz, HALF, 256 - HALF), ydev)
        to_sibling("sB", 1, dz)

    def norm_block(i, carry):
        rows = pl.ds(pl.multiple_of(i * 32, 32), 32)
        acc = jnp.zeros((32, 512), F32)
        for j in range(16):
            h = hid[rows, j * 512:(j + 1) * 512].astype(F32)
            acc = acc + h * h
        total = jnp.sum(acc, axis=-1, keepdims=True)
        s = lax.rsqrt(total / D + epsilon)
        scl[rows, :] = s
        for j in range(16):
            h = hid[rows, j * 512:(j + 1) * 512].astype(F32)
            g = gain[:, j * 512:(j + 1) * 512].astype(F32)
            n = (h * s * g).astype(BF16)
            nrm[0, rows, j * 256:(j + 1) * 256] = n[:, :256]
            nrm[1, rows, j * 256:(j + 1) * 256] = n[:, 256:]
        return carry

    def step_norm(i):
        if i == 0:
            local[3].wait()
        local[4 + i].wait()
        lax.fori_loop(i * 4, i * 4 + 4, norm_block, 0)
        rows = pl.ds(i * 128, 128)
        send(("n", i), nrm.at[1 - c, rows], nsib.at[rows], sdev)

    def step_part(p):
        if p == 0:
            arrive(("n",), w.at[pl.ds(0, 2304)], sdev)
            cot_t[1] = cot[1].T
        first, second = GROUPS[p]

        def one(i, carry):
            zz = lax.rem(z + NZ + first + (second - first) * lax.div(i, 2), NZ)
            q = lax.rem(y + lax.rem(i, 2), 2) * NZ + zz
            cols = pl.ds(pl.multiple_of(q * 256, 256), 256)
            a = jnp.dot(cot_t[0], nrm[c, :, cols], preferred_element_type=F32)
            b = jnp.dot(cot_t[1], nsib[:, cols], preferred_element_type=F32)
            part[q] = a + b
            return carry

        lax.fori_loop(0, 4, one, 0)

    def work_on(q):
        cols = pl.ds(pl.multiple_of(q * 512, 512), 512)
        half = pl.ds(pl.multiple_of(q * 256, 256), 256)
        rows = pl.multiple_of(q * 512, 512)
        w0 = w[pl.ds(rows, 256), :]
        w1 = w[pl.ds(rows + 256, 256), :]
        kacc[...] += jnp.dot(nrm[0, :, half], w0, preferred_element_type=F32) + jnp.dot(
            nrm[1, :, half], w1, preferred_element_type=F32
        )
        back = lax.dot_general(
            cot[0], w[pl.ds(rows, 512), :], (((1,), (1,)), ((), ())), preferred_element_type=F32
        )
        u = back * gain[:, cols].astype(F32)
        upper[:, cols] = u
        t = u * hid[:, cols].astype(F32)
        iacc[...] += (t[:, :128] + t[:, 128:256]) + (t[:, 256:384] + t[:, 384:])

    def step_pair(dz):
        arrive(("s", dz), w.at[pl.ds(pl.multiple_of(q_of(0, dz) * 512, 512), 512)], sdev)

        def one(i, carry):
            work_on(lax.rem(y + i, 2) * NZ + lax.rem(z + NZ + dz, NZ))
            return carry

        lax.fori_loop(0, 2, one, 0)

    def add_into(dst, terms, rows, step=64):
        def one(i, carry):
            r = pl.ds(pl.multiple_of(i * step, step), step)
            total = terms[0][r, :].astype(F32)
            for term in terms[1:]:
                total = total + term[r, :].astype(F32)
            dst[r, :] = total.astype(dst.dtype)
            return carry

        lax.fori_loop(0, rows // step, one, 0)

    def p_rows(dy, dz, start, size):
        return part.at[q_of(dy, dz), pl.ds(start, size)]

    def step_ryb(dz):
        slot = dz + 3
        add_into(yb_s.at[slot], [p_rows(1, dz, 256, 256)], 256)
        send(("ryB", dz), yb_s.at[slot], yb_r.at[slot], ydev)

    def step_ra(d, dy, t):
        dz = norm_dz(SIGNS[d] * (5 - t))
        mine = p_rows(dy, dz, 0, 256)
        if t == 5 - chain_len(d, dy):
            buf = st_a.at[d, dy]
            add_into(buf, [mine], 256)
        else:
            buf = r_a.at[d, dy, t - 2]
            arrive(("rA", d, dy, t - 1), buf, zdev[d])
            add_into(buf, [buf, mine], 256)
        send(("rA", d, dy, t), buf, r_a.at[d, dy, t - 1], zdev[d])

    def arrive_yb(dz):
        arrive(("ryB", dz), yb_r.at[dz + 3], ydev)

    def step_rb(d, t):
        dz = norm_dz(SIGNS[d] * (5 - t))
        slot = dz + 3
        start = d * 128
        other = 128 - start
        if t == 1:
            if not seen:
                arrive_yb(dz)
                seen.append(dz)
            add_into(
                st_b.at[d],
                [p_rows(0, dz, 256 + start, 128), yb_r.at[slot, pl.ds(start, 128)]], 128,
            )
            send(("rB", d, 1), st_b.at[d], r_b.at[d, 0, pl.ds(start, 128)], zdev[d])
            return
        arrive_yb(dz)
        buf = r_b.at[d, t - 2]
        if t == 2:
            arrive(("rB", d, 1), buf.at[pl.ds(start, 128)], zdev[d])
            add_into(
                buf.at[pl.ds(other, 128)],
                [p_rows(0, dz, 256 + other, 128), yb_r.at[slot, pl.ds(other, 128)]], 128,
            )
            add_into(
                buf.at[pl.ds(start, 128)],
                [buf.at[pl.ds(start, 128)], p_rows(0, dz, 256 + start, 128), yb_r.at[slot, pl.ds(start, 128)]],
                128,
            )
        else:
            arrive(("rB", d, t - 1), buf, zdev[d])
            add_into(buf, [buf, p_rows(0, dz, 256, 256), yb_r.at[slot]], 256)
        send(("rB", d, t), buf, r_b.at[d, t - 1], zdev[d])

    seen = []

    def last_a(dy):
        arrive(("rA", 4, dy), w.at[pl.ds(0, 256)], zdev[0])
        return [p_rows(dy, 0, 0, 256), r_a.at[0, dy, 3], r_a.at[1, dy, 3]]

    def write_gw(start, terms):
        for i in range(2):
            r = slice(i * 128, (i + 1) * 128)
            total = terms[0][r, :].astype(F32)
            for term in terms[1:]:
                total = total + term[r, :].astype(F32)
            gw_o[0, :, start + i * 128:start + (i + 1) * 128] = total.T

    def step_rya():
        add_into(ya_s, last_a(1), 256)
        send(("ryA",), ya_s, ya_r, ydev)

    def step_end_b():
        arrive_yb(0)
        arrive(("rB", 4), w.at[pl.ds(0, 256)], zdev[0])
        write_gw(256, [p_rows(0, 0, 256, 256), yb_r.at[3], r_b.at[0, 3], r_b.at[1, 3]])

    def step_end_a():
        terms = last_a(0)
        arrive(("ryA",), ya_r, ydev)
        write_gw(0, terms + [ya_r])

    mine64 = pl.ds(pl.multiple_of(x * 64, 64), 64)

    def step_fx():
        arrive(("fx",), w.at[pl.ds(0, 192)], xdev[1])
        others = [fx[j].astype(F32) for j in range(3)]
        fs[0] = (fl[mine64, :].astype(F32) + others[1]) + (others[0] + others[2])
        send(("fy",), fs.at[0], fs.at[1], ydev)

    def step_fy():
        arrive(("fy",), fs.at[1], ydev)
        send(("fz",), fs.at[1], fs.at[2], hdev)

    def step_fz():
        arrive(("fz",), fs.at[2], hdev)
        ftot[mine64, :] = (fs[0] + fs[2]) / ISLANDS
        for j in (1, 2, 3):
            send(("ft", j), ftot.at[mine64], ftot.at[mine64], xdev[j])

    def step_ft():
        arrive(("ft",), ftot.at[pl.ds(0, 192)], xdev[1])
        local[6].wait()
        local[7].wait()

        def outer(i, carry):
            r = pl.ds(pl.multiple_of(i * 32, 32), 32)
            g = fg[r, :]
            pseudo = g - ftot[r, :]
            moment = outer_momentum * fm[r, :] + pseudo
            new = g - outer_rate * (pseudo + outer_momentum * moment)
            nm_o[r, :] = moment
            ng_o[r, :] = new
            nl_o[0, r, :] = (mix_weight * fl[r, :].astype(F32) + (1.0 - mix_weight) * new).astype(BF16)
            return carry

        lax.fori_loop(0, 8, outer, 0)

    def step_fin(p):
        if p == 0:
            keys_o[0] = kacc[...].astype(BF16)

        def finish(i, carry):
            r = pl.ds(pl.multiple_of(i * 32, 32), 32)
            s = scl[r, :]
            inner = jnp.sum(iacc[r, :], axis=-1, keepdims=True) / D
            coef = s * s * s * inner
            for j in range(16):
                cols = slice(j * 512, (j + 1) * 512)
                gi_o[0, r, cols] = (s * upper[r, cols] - hid[r, cols].astype(F32) * coef).astype(BF16)
            return carry

        lax.fori_loop(2 * p, 2 * p + 2, finish, 0)

    steps = {
        "start": step_start, "gyA": step_gya, "gA": step_ga, "gB": step_gb, "gyB": step_gyb,
        "norm": step_norm, "part": step_part, "ryB": step_ryb, "rA": step_ra, "rB": step_rb,
        "fx": step_fx, "fy": step_fy, "fz": step_fz, "ft": step_ft, "pair": step_pair, "fin": step_fin,
        "ryA": step_rya, "endB": step_end_b, "endA": step_end_a,
    }
    for step in ORDER:
        steps[step[0]](*step[1:])

    for group in (0, 1):
        everything = w.at[pl.ds(0, sent[group] // (KC * 2))]
        pltpu.make_async_remote_copy(
            src_ref=everything, dst_ref=everything, send_sem=ssem.at[group], recv_sem=rsem.at[0],
            device_id=sdev, device_id_type=MESH,
        ).wait_send()


def store(*refs):
    n = (len(refs) - 1) // 2
    copies = [pltpu.make_async_copy(refs[i], refs[n + i], refs[-1].at[i]) for i in range(n)]
    for copy in copies:
        copy.start()
    for copy in copies:
        copy.wait()


def body(*args):
    outs = [
        ((1, TOK, KC), BF16),
        ((1, TOK, D), BF16),
        ((1, TOK, KC), F32),
        ((TOK, KC), F32),
        ((TOK, KC), F32),
        ((1, TOK, KC), BF16),
    ]
    vm = pltpu.VMEM
    results = pl.pallas_call(
        kernel,
        out_shape=[vm(*o) for o in outs],
        in_specs=[pl.BlockSpec(memory_space=pltpu.HBM)] * 7,
        out_specs=[pl.BlockSpec(memory_space=vm)] * 6,
        scratch_shapes=[
            vm((D, KC), BF16),
            vm((TOK, D), BF16),
            vm((2, TOK, D // 2), BF16),
            vm((TOK, D // 2), BF16),
            vm((TOK, D), F32),
            vm((NCHIP, KC, 256), F32),
            vm((1, D), BF16),
            vm((2, TOK, KC), BF16),
            vm((2, KC, TOK), BF16),
            vm((TOK, KC), F32),
            vm((TOK, 128), F32),
            vm((TOK, 1), F32),
            vm((TOK, KC), F32),
            vm((TOK, KC), F32),
            vm((TOK, KC), BF16),
            vm((3, 64, KC), BF16),
            vm((3, 64, KC), F32),
            vm((TOK, KC), F32),
            vm((2, 2, 4, 256, 256), BF16),
            vm((2, 2, 256, 256), BF16),
            vm((8, 256, 256), BF16),
            vm((8, 256, 256), BF16),
            vm((2, 4, 256, 256), BF16),
            vm((2, 128, 256), BF16),
            vm((256, 256), BF16),
            vm((256, 256), BF16),
            pltpu.SemaphoreType.DMA((2,)),
            pltpu.SemaphoreType.DMA((len(ARRIVALS),)),
            pltpu.SemaphoreType.DMA((8,)),
        ],
        compiler_params=pltpu.CompilerParams(
            collective_id=0, has_side_effects=True, vmem_limit_bytes=56 * 2**20
        ),
    )(*args)
    return tuple(
        pl.pallas_call(
            store,
            out_shape=[jax.ShapeDtypeStruct(*o) for o in outs],
            in_specs=[pl.BlockSpec(memory_space=pl.ANY)] * 6,
            out_specs=[pl.BlockSpec(memory_space=pl.ANY)] * 6,
            scratch_shapes=[pltpu.SemaphoreType.DMA((6,))],
            compiler_params=pltpu.CompilerParams(vmem_limit_bytes=2**20),
        )(*results)
    )


def solution(mesh):
    rows = P("island", "fsdp", None)
    frag = P("fsdp", None)
    return jax.shard_map(
        body,
        mesh=mesh,
        in_specs=(rows, P("island", None), rows, rows, frag, frag, rows),
        out_specs=(rows, rows, rows, frag, frag, rows),
        check_vma=False,
    )
```

```python
import math

import jax
import jax.numpy as jnp
from jax import lax
from jax.experimental import pallas as pl
from jax.experimental.pallas import tpu as pltpu
from jax.sharding import PartitionSpec as P

epsilon = 1e-05
outer_rate = 0.7
outer_momentum = 0.9
mix_weight = 0.5

MESH = pl.DeviceIdType.MESH
F32 = jnp.float32
BF16 = jnp.bfloat16

D = 8192
KC = 512
TOK = 256
NZ = 8
ISLANDS = 8
NCHIP = 16
HALF = 112
RA = 240
RB = KC - RA
RB0 = RB // 32 * 16 + RB % 32
SIGNS = (1, -1)


def norm_dz(dz):
    dz = dz % NZ
    return dz - NZ if dz > 4 else dz


def chain_len(d, dy):
    return 4 if d == dy else 3


def arrival(name):
    kind = name[0]
    if kind in ("own", "sA", "sB"):
        return ("s", name[2] if len(name) > 1 else 0)
    if kind in ("cot", "n"):
        return ("n",)
    if kind in ("fx", "ft"):
        return (kind,)
    if kind in ("gB", "rB") and name[2] == 4:
        return (kind, 4)
    if kind == "rA" and name[3] == 4:
        return (kind, 4, name[2])
    return name


def arrivals():
    names = [("gyA",), ("ryA",), ("n",), ("fx",), ("fy",), ("fz",), ("ft",), ("gB", 4), ("rB", 4)]
    for dy in (0, 1):
        names += [("rA", 4, dy)]
        for d in (0, 1):
            names += [("gA", d, dy, k) for k in range(1, 1 + chain_len(d, dy))]
            names += [("rA", d, dy, t) for t in range(5 - chain_len(d, dy), 4)]
    for k in (1, 2, 3):
        names += [(kind, d, k) for kind in ("gB", "rB") for d in (0, 1)]
    for dz in range(-3, 5):
        names += [(kind, dz) for kind in ("gyB", "ryB", "s")]
    return {name: i for i, name in enumerate(names)}


ARRIVALS = arrivals()

ORDER = (
    ("start",), ("norm", 0), ("norm", 1), ("gyA",), ("gB", 0, 1), ("gB", 1, 1), ("gA", 1, 0, 1), ("gA", 0, 1, 1),
    ("fx",), ("part", 0), ("gA", 0, 0, 1), ("rA", 0, 0, 1), ("rA", 1, 1, 1), ("ryB", 4), ("gA", 1, 1, 1), ("part", 1),
    ("gB", 1, 2), ("gyB", 0), ("gB", 0, 2), ("gA", 0, 1, 2), ("gyB", -1), ("gyB", 1), ("fy",), ("part", 2),
    ("gA", 1, 0, 2), ("ryB", -3), ("rA", 0, 0, 2), ("gA", 0, 0, 2), ("pair", -1), ("rA", 0, 1, 2), ("gA", 1, 1, 2),
    ("rA", 1, 0, 2), ("gB", 1, 3), ("fz",), ("pair", 0), ("gA", 0, 1, 3), ("ryB", 3), ("gyB", -2), ("gyB", 2),
    ("rA", 1, 1, 2), ("rB", 0, 1), ("rB", 1, 1), ("gA", 1, 1, 3), ("gB", 0, 3), ("rA", 0, 1, 3), ("pair", 1),
    ("rB", 0, 2), ("ryB", -2), ("gyB", 3), ("rA", 1, 1, 3), ("gB", 1, 4), ("gA", 0, 0, 3), ("rA", 1, 0, 3),
    ("gyB", -3), ("ryB", 2), ("gA", 1, 0, 3), ("rB", 1, 2), ("rA", 0, 1, 4), ("gA", 1, 1, 4), ("part", 3), ("ft",),
    ("ryB", -1), ("rA", 1, 1, 4), ("pair", 3), ("rA", 0, 0, 3), ("pair", -2), ("rB", 1, 3), ("ryB", 1), ("rB", 0, 3),
    ("gA", 0, 0, 4), ("rA", 1, 0, 4), ("gyB", 4), ("ryA",), ("rA", 0, 0, 4), ("ryB", 0), ("pair", -3), ("pair", 4),
    ("rB", 1, 4), ("rB", 0, 4), ("pair", 2), ("fin", 0), ("fin", 1), ("endA",), ("fin", 2), ("fin", 3), ("endB",),
)

GROUPS = ((4, 3), (-3, 2), (-2, 1), (-1, 0))


def kernel(
    hid_h, gain_h, w_h, cot_h, fg_h, fm_h, fl_h,
    keys_o, gi_o, gw_o, ng_o, nm_o, nl_o,
    w, hid, nrm, nsib, upper, part, gain, cot, cot_t, kacc, iacc, scl,
    fg, fm, fl, fx, fs, ftot,
    r_a, st_a, yb_s, yb_r, r_b, st_b, ya_s, ya_r,
    ssem, rsem, lsem,
):
    island = lax.axis_index("island")
    f = lax.axis_index("fsdp")
    c = lax.rem(f, 2)
    z = lax.rem(lax.div(f, 2), NZ)
    y = lax.div(f, 2 * NZ)
    x = lax.rem(island, 4)
    yh = lax.div(island, 4)

    def fsdp_of(yy, zz, cc):
        return (yy * NZ + zz) * 2 + cc

    def q_of(dy, dz):
        yy = y if dy == 0 else 1 - y
        return yy * NZ + lax.rem(z + (dz + NZ), NZ)

    zdev = [
        (island, fsdp_of(y, lax.rem(z + 1, NZ), c)),
        (island, fsdp_of(y, lax.rem(z + NZ - 1, NZ), c)),
    ]
    ydev = (island, fsdp_of(1 - y, z, c))
    sdev = (island, fsdp_of(y, z, 1 - c))
    xdev = {j: (yh * 4 + lax.rem(x + j, 4), f) for j in (1, 2, 3)}
    hdev = ((1 - yh) * 4 + x, fsdp_of(1 - y, z, c))
    peers = zdev + [ydev, sdev, hdev] + [xdev[j] for j in (1, 2, 3)]

    sent = [0, 0]

    def send(name, src, dst, dev):
        group = 0 if name[0] in ("own", "gA", "gB", "gyA", "gyB", "sA", "sB") else 1
        pltpu.make_async_remote_copy(
            src_ref=src, dst_ref=dst, send_sem=ssem.at[group], recv_sem=rsem.at[ARRIVALS[arrival(name)]],
            device_id=dev, device_id_type=MESH,
        ).start()
        sent[group] += math.prod(src.shape) * src.dtype.itemsize

    def arrive(name, ref, dev):
        pltpu.make_async_remote_copy(
            src_ref=ref, dst_ref=ref, send_sem=ssem.at[0], recv_sem=rsem.at[ARRIVALS[name]],
            device_id=dev, device_id_type=MESH,
        ).wait_recv()

    loads = [
        (w_h.at[0], w.at[pl.ds(pl.multiple_of((y * NZ + z) * 512 + c * 256, 256), 256)]),
        (cot_h.at[0], cot.at[0]),
        (fl_h.at[0], fl),
        (gain_h, gain),
        (hid_h.at[0, pl.ds(0, 128)], hid.at[pl.ds(0, 128)]),
        (hid_h.at[0, pl.ds(128, 128)], hid.at[pl.ds(128, 128)]),
        (fg_h, fg),
        (fm_h, fm),
    ]
    local = [pltpu.make_async_copy(s, t, lsem.at[i]) for i, (s, t) in enumerate(loads)]
    for copy in local:
        copy.start()

    barrier = pltpu.get_barrier_semaphore()
    for dev in peers:
        pl.semaphore_signal(barrier, inc=1, device_id=dev, device_id_type=MESH)
    pl.semaphore_wait(barrier, len(peers))

    def wrows(dy, dz, start, size, core=None):
        core = c if core is None else core
        row = q_of(dy, dz) * 512 + core * 256 + start
        return w.at[pl.ds(pl.multiple_of(row, 16), size)]

    def b_span(d, k):
        if k < 4:
            return HALF, 256 - HALF
        half = (256 - HALF) // 32 * 16
        first = 256 - HALF - half
        return (HALF, first) if d == 0 else (HALF + first, half)

    def g_send_a(d, dy, k):
        part_ = wrows(dy, norm_dz(-SIGNS[d] * (k - 1)), 0, HALF)
        send(("gA", d, dy, k), part_, part_, zdev[d])

    def g_send_b(d, k):
        start, size = b_span(d, k)
        part_ = wrows(0, norm_dz(-SIGNS[d] * (k - 1)), start, size)
        send(("gB", d, k), part_, part_, zdev[d])

    def g_send_yb(dz):
        part_ = wrows(0, dz, HALF, 256 - HALF)
        send(("gyB", dz), part_, part_, ydev)

    def to_sibling(which, dy, dz):
        start, size = (0, HALF) if which == "sA" else (HALF, 256 - HALF)
        part_ = wrows(dy, dz, start, size)
        send((which, dy, dz), part_, part_, sdev)

    def step_start():
        for i in range(2):
            local[i].wait()
        send(("gyA",), wrows(0, 0, 0, HALF), wrows(0, 0, 0, HALF), ydev)
        for d in (0, 1):
            g_send_b(d, 1)
        g_send_yb(0)
        for d in (0, 1):
            g_send_a(d, 0, 1)
        send(("own",), wrows(0, 0, 0, 256), wrows(0, 0, 0, 256), sdev)
        send(("cot",), cot.at[0], cot.at[1], sdev)
        local[2].wait()
        for j in (1, 2, 3):
            quarter = pl.ds(pl.multiple_of(lax.rem(x + j, 4) * 64, 64), 64)
            send(("fx", j), fl.at[quarter], fx.at[j - 1], xdev[j])
        kacc[...] = jnp.zeros_like(kacc)
        iacc[...] = jnp.zeros_like(iacc)
        cot_t[0] = cot[0].T

    def step_gya():
        arrive(("gyA",), wrows(1, 0, 0, HALF), ydev)
        for d in (0, 1):
            g_send_a(d, 1, 1)
        to_sibling("sA", 1, 0)

    def step_ga(d, dy, k):
        dz = norm_dz(-SIGNS[d] * k)
        arrive(("gA", d, dy, k), wrows(dy, dz, 0, HALF), zdev[d])
        if k < chain_len(d, dy):
            g_send_a(d, dy, k + 1)
        to_sibling("sA", dy, dz)

    def step_gb(d, k):
        dz = norm_dz(-SIGNS[d] * k)
        if k == 4:
            arrive(("gB", 4), wrows(0, dz, HALF, 256 - HALF), zdev[d])
        else:
            arrive(("gB", d, k), wrows(0, dz, HALF, 256 - HALF), zdev[d])
            g_send_b(d, k + 1)
        g_send_yb(dz)
        to_sibling("sB", 0, dz)

    def step_gyb(dz):
        arrive(("gyB", dz), wrows(1, dz, HALF, 256 - HALF), ydev)
        to_sibling("sB", 1, dz)

    def norm_block(i, carry):
        rows = pl.ds(pl.multiple_of(i * 32, 32), 32)
        acc = jnp.zeros((32, 512), F32)
        for j in range(16):
            h = hid[rows, j * 512:(j + 1) * 512].astype(F32)
            acc = acc + h * h
        total = jnp.sum(acc, axis=-1, keepdims=True)
        s = lax.rsqrt(total / D + epsilon)
        scl[rows, :] = s
        for j in range(16):
            h = hid[rows, j * 512:(j + 1) * 512].astype(F32)
            g = gain[:, j * 512:(j + 1) * 512].astype(F32)
            n = (h * s * g).astype(BF16)
            nrm[0, rows, j * 256:(j + 1) * 256] = n[:, :256]
            nrm[1, rows, j * 256:(j + 1) * 256] = n[:, 256:]
        return carry

    def step_norm(i):
        if i == 0:
            local[3].wait()
        local[4 + i].wait()
        lax.fori_loop(i * 4, i * 4 + 4, norm_block, 0)
        rows = pl.ds(i * 128, 128)
        send(("n", i), nrm.at[1 - c, rows], nsib.at[rows], sdev)

    def step_part(p):
        if p == 0:
            arrive(("n",), w.at[pl.ds(0, 2304)], sdev)
            cot_t[1] = cot[1].T
        first, second = GROUPS[p]

        def one(i, carry):
            zz = lax.rem(z + NZ + first + (second - first) * lax.div(i, 2), NZ)
            q = lax.rem(y + lax.rem(i, 2), 2) * NZ + zz
            cols = pl.ds(pl.multiple_of(q * 256, 256), 256)
            a = jnp.dot(cot_t[0], nrm[c, :, cols], preferred_element_type=F32)
            b = jnp.dot(cot_t[1], nsib[:, cols], preferred_element_type=F32)
            part[q] = a + b
            return carry

        lax.fori_loop(0, 4, one, 0)

    def work_on(q):
        cols = pl.ds(pl.multiple_of(q * 512, 512), 512)
        half = pl.ds(pl.multiple_of(q * 256, 256), 256)
        rows = pl.multiple_of(q * 512, 512)
        w0 = w[pl.ds(rows, 256), :]
        w1 = w[pl.ds(rows + 256, 256), :]
        kacc[...] += jnp.dot(nrm[0, :, half], w0, preferred_element_type=F32) + jnp.dot(
            nrm[1, :, half], w1, preferred_element_type=F32
        )
        back = lax.dot_general(
            cot[0], w[pl.ds(rows, 512), :], (((1,), (1,)), ((), ())), preferred_element_type=F32
        )
        u = back * gain[:, cols].astype(F32)
        upper[:, cols] = u
        t = u * hid[:, cols].astype(F32)
        iacc[...] += (t[:, :128] + t[:, 128:256]) + (t[:, 256:384] + t[:, 384:])

    def step_pair(dz):
        arrive(("s", dz), w.at[pl.ds(pl.multiple_of(q_of(0, dz) * 512, 512), 512)], sdev)

        def one(i, carry):
            work_on(lax.rem(y + i, 2) * NZ + lax.rem(z + NZ + dz, NZ))
            return carry

        lax.fori_loop(0, 2, one, 0)

    def add_into(dst, terms, rows):
        def some(r):
            total = terms[0][r, :].astype(F32)
            for term in terms[1:]:
                total = total + term[r, :].astype(F32)
            dst[r, :] = total.astype(dst.dtype)

        def one(i, carry):
            some(pl.ds(pl.multiple_of(i * 64, 64), 64))
            return carry

        lax.fori_loop(0, rows // 64, one, 0)
        if rows % 64:
            some(pl.ds(rows // 64 * 64, rows % 64))

    def p_rows(dy, dz, start, size):
        return part.at[q_of(dy, dz), pl.ds(start, size)]

    def step_ryb(dz):
        slot = dz + 3
        add_into(yb_s.at[slot], [p_rows(1, dz, RA, RB)], RB)
        send(("ryB", dz), yb_s.at[slot], yb_r.at[slot], ydev)

    def step_ra(d, dy, t):
        dz = norm_dz(SIGNS[d] * (5 - t))
        mine = p_rows(dy, dz, 0, RA)
        if t == 5 - chain_len(d, dy):
            buf = st_a.at[d, dy]
            add_into(buf, [mine], RA)
        else:
            buf = r_a.at[d, dy, t - 2]
            arrive(("rA", d, dy, t - 1), buf, zdev[d])
            add_into(buf, [buf, mine], RA)
        send(("rA", d, dy, t), buf, r_a.at[d, dy, t - 1], zdev[d])

    def arrive_yb(dz):
        arrive(("ryB", dz), yb_r.at[dz + 3], ydev)

    def step_rb(d, t):
        dz = norm_dz(SIGNS[d] * (5 - t))
        slot = dz + 3
        spans = ((0, RB0), (RB0, RB - RB0))
        start, size = spans[d]
        span = pl.ds(start, size)
        if t == 1:
            if not seen:
                arrive_yb(dz)
                seen.append(dz)
            buf = st_b.at[d, pl.ds(0, size)]
            add_into(buf, [p_rows(0, dz, RA + start, size), yb_r.at[slot, span]], size)
            send(("rB", d, 1), buf, r_b.at[d, 0, span], zdev[d])
            return
        arrive_yb(dz)
        buf = r_b.at[d, t - 2]
        if t == 2:
            arrive(("rB", d, 1), buf.at[span], zdev[d])
            add_into(buf.at[span], [buf.at[span], p_rows(0, dz, RA + start, size), yb_r.at[slot, span]], size)
            start, size = spans[1 - d]
            span = pl.ds(start, size)
            add_into(buf.at[span], [p_rows(0, dz, RA + start, size), yb_r.at[slot, span]], size)
        else:
            arrive(("rB", d, t - 1), buf, zdev[d])
            add_into(buf, [buf, p_rows(0, dz, RA, RB), yb_r.at[slot]], RB)
        send(("rB", d, t), buf, r_b.at[d, t - 1], zdev[d])

    seen = []

    def last_a(dy):
        arrive(("rA", 4, dy), w.at[pl.ds(0, RA)], zdev[0])
        return [p_rows(dy, 0, 0, RA), r_a.at[0, dy, 3], r_a.at[1, dy, 3]]

    ended = []

    def write_gw(block, terms, start, size):
        mine = part.at[q_of(0, 0)]
        add_into(mine.at[pl.ds(start, size)], terms, size)
        blocks = (0,) if block == 0 else (2, 3)
        for i in blocks + ((1,) if ended else ()):
            gw_o[0, :, i * 128:(i + 1) * 128] = mine[pl.ds(i * 128, 128), :].T
        ended.append(block)

    def step_rya():
        add_into(ya_s, last_a(1), RA)
        send(("ryA",), ya_s, ya_r, ydev)

    def step_end_b():
        arrive_yb(0)
        arrive(("rB", 4), w.at[pl.ds(0, RB)], zdev[0])
        write_gw(2, [p_rows(0, 0, RA, RB), yb_r.at[3], r_b.at[0, 3], r_b.at[1, 3]], RA, RB)

    def step_end_a():
        terms = last_a(0)
        arrive(("ryA",), ya_r, ydev)
        write_gw(0, terms + [ya_r], 0, RA)

    mine64 = pl.ds(pl.multiple_of(x * 64, 64), 64)

    def step_fx():
        arrive(("fx",), w.at[pl.ds(0, 192)], xdev[1])
        others = [fx[j].astype(F32) for j in range(3)]
        fs[0] = (fl[mine64, :].astype(F32) + others[1]) + (others[0] + others[2])
        send(("fy",), fs.at[0], fs.at[1], ydev)

    def step_fy():
        arrive(("fy",), fs.at[1], ydev)
        send(("fz",), fs.at[1], fs.at[2], hdev)

    def step_fz():
        arrive(("fz",), fs.at[2], hdev)
        ftot[mine64, :] = (fs[0] + fs[2]) / ISLANDS
        for j in (1, 2, 3):
            send(("ft", j), ftot.at[mine64], ftot.at[mine64], xdev[j])

    def step_ft():
        arrive(("ft",), ftot.at[pl.ds(0, 192)], xdev[1])
        local[6].wait()
        local[7].wait()

        def outer(i, carry):
            r = pl.ds(pl.multiple_of(i * 32, 32), 32)
            g = fg[r, :]
            pseudo = g - ftot[r, :]
            moment = outer_momentum * fm[r, :] + pseudo
            new = g - outer_rate * (pseudo + outer_momentum * moment)
            nm_o[r, :] = moment
            ng_o[r, :] = new
            nl_o[0, r, :] = (mix_weight * fl[r, :].astype(F32) + (1.0 - mix_weight) * new).astype(BF16)
            return carry

        lax.fori_loop(0, 8, outer, 0)

    def step_fin(p):
        if p == 0:
            keys_o[0] = kacc[...].astype(BF16)

        def finish(i, carry):
            r = pl.ds(pl.multiple_of(i * 32, 32), 32)
            s = scl[r, :]
            inner = jnp.sum(iacc[r, :], axis=-1, keepdims=True) / D
            coef = s * s * s * inner
            for j in range(16):
                cols = slice(j * 512, (j + 1) * 512)
                gi_o[0, r, cols] = (s * upper[r, cols] - hid[r, cols].astype(F32) * coef).astype(BF16)
            return carry

        lax.fori_loop(2 * p, 2 * p + 2, finish, 0)

    steps = {
        "start": step_start, "gyA": step_gya, "gA": step_ga, "gB": step_gb, "gyB": step_gyb,
        "norm": step_norm, "part": step_part, "ryB": step_ryb, "rA": step_ra, "rB": step_rb,
        "fx": step_fx, "fy": step_fy, "fz": step_fz, "ft": step_ft, "pair": step_pair, "fin": step_fin,
        "ryA": step_rya, "endB": step_end_b, "endA": step_end_a,
    }
    for step in ORDER:
        steps[step[0]](*step[1:])

    for group in (0, 1):
        everything = w.at[pl.ds(0, sent[group] // (KC * 2))]
        pltpu.make_async_remote_copy(
            src_ref=everything, dst_ref=everything, send_sem=ssem.at[group], recv_sem=rsem.at[0],
            device_id=sdev, device_id_type=MESH,
        ).wait_send()


def store(*refs):
    n = (len(refs) - 1) // 2
    copies = [pltpu.make_async_copy(refs[i], refs[n + i], refs[-1].at[i]) for i in range(n)]
    for copy in copies:
        copy.start()
    for copy in copies:
        copy.wait()


def body(*args):
    outs = [
        ((1, TOK, KC), BF16),
        ((1, TOK, D), BF16),
        ((1, TOK, KC), F32),
        ((TOK, KC), F32),
        ((TOK, KC), F32),
        ((1, TOK, KC), BF16),
    ]
    vm = pltpu.VMEM
    results = pl.pallas_call(
        kernel,
        out_shape=[vm(*o) for o in outs],
        in_specs=[pl.BlockSpec(memory_space=pltpu.HBM)] * 7,
        out_specs=[pl.BlockSpec(memory_space=vm)] * 6,
        scratch_shapes=[
            vm((D, KC), BF16),
            vm((TOK, D), BF16),
            vm((2, TOK, D // 2), BF16),
            vm((TOK, D // 2), BF16),
            vm((TOK, D), F32),
            vm((NCHIP, KC, 256), F32),
            vm((1, D), BF16),
            vm((2, TOK, KC), BF16),
            vm((2, KC, TOK), BF16),
            vm((TOK, KC), F32),
            vm((TOK, 128), F32),
            vm((TOK, 1), F32),
            vm((TOK, KC), F32),
            vm((TOK, KC), F32),
            vm((TOK, KC), BF16),
            vm((3, 64, KC), BF16),
            vm((3, 64, KC), F32),
            vm((TOK, KC), F32),
            vm((2, 2, 4, RA, 256), BF16),
            vm((2, 2, RA, 256), BF16),
            vm((8, RB, 256), BF16),
            vm((8, RB, 256), BF16),
            vm((2, 4, RB, 256), BF16),
            vm((2, RB0, 256), BF16),
            vm((RA, 256), BF16),
            vm((RA, 256), BF16),
            pltpu.SemaphoreType.DMA((2,)),
            pltpu.SemaphoreType.DMA((len(ARRIVALS),)),
            pltpu.SemaphoreType.DMA((8,)),
        ],
        compiler_params=pltpu.CompilerParams(
            collective_id=0, has_side_effects=True, vmem_limit_bytes=56 * 2**20
        ),
    )(*args)
    return tuple(
        pl.pallas_call(
            store,
            out_shape=[jax.ShapeDtypeStruct(*o) for o in outs],
            in_specs=[pl.BlockSpec(memory_space=pl.ANY)] * 6,
            out_specs=[pl.BlockSpec(memory_space=pl.ANY)] * 6,
            scratch_shapes=[pltpu.SemaphoreType.DMA((6,))],
            compiler_params=pltpu.CompilerParams(vmem_limit_bytes=2**20),
        )(*results)
    )


def solution(mesh):
    rows = P("island", "fsdp", None)
    frag = P("fsdp", None)
    return jax.shard_map(
        body,
        mesh=mesh,
        in_specs=(rows, P("island", None), rows, rows, frag, frag, rows),
        out_specs=(rows, rows, rows, frag, frag, rows),
        check_vma=False,
    )
```

```python
import math

import jax
import jax.numpy as jnp
from jax import lax
from jax.experimental import pallas as pl
from jax.experimental.pallas import tpu as pltpu
from jax.sharding import PartitionSpec as P

epsilon = 1e-05
outer_rate = 0.7
outer_momentum = 0.9
mix_weight = 0.5

MESH = pl.DeviceIdType.MESH
F32 = jnp.float32
BF16 = jnp.bfloat16

D = 8192
KC = 512
TOK = 256
NZ = 8
ISLANDS = 8
NCHIP = 16
HALF = 112
RA = 240
RB = KC - RA
RB0 = RB // 32 * 16 + RB % 32
SIGNS = (1, -1)


def norm_dz(dz):
    dz = dz % NZ
    return dz - NZ if dz > 4 else dz


def chain_len(d, dy):
    return 4 if d == dy else 3


def arrival(name):
    kind = name[0]
    if kind in ("own", "sA", "sB"):
        return ("s", name[2] if len(name) > 1 else 0)
    if kind in ("cot", "n"):
        return ("n",)
    if kind in ("fx", "ft"):
        return (kind,)
    if kind in ("gB", "rB") and name[2] == 4:
        return (kind, 4)
    if kind == "rA" and name[3] == 4:
        return (kind, 4, name[2])
    return name


def arrivals():
    names = [("gyA",), ("ryA",), ("n",), ("fx",), ("fy",), ("fz",), ("ft",), ("gB", 4), ("rB", 4)]
    for dy in (0, 1):
        names += [("rA", 4, dy)]
        for d in (0, 1):
            names += [("gA", d, dy, k) for k in range(1, 1 + chain_len(d, dy))]
            names += [("rA", d, dy, t) for t in range(5 - chain_len(d, dy), 4)]
    for k in (1, 2, 3):
        names += [(kind, d, k) for kind in ("gB", "rB") for d in (0, 1)]
    for dz in range(-3, 5):
        names += [(kind, dz) for kind in ("gyB", "ryB", "s")]
    return {name: i for i, name in enumerate(names)}


ARRIVALS = arrivals()

ORDER = (
    ("start",), ("norm", 0), ("tin", 0), ("norm", 1), ("tin", 1), ("gB", 0, 1), ("gB", 1, 1), ("tin", 2),
    ("gA", 1, 0, 1), ("tin", 3), ("gyB", 0), ("gyA",), ("gA", 0, 0, 1), ("far",), ("gB", 0, 2), ("gB", 1, 2),
    ("part", 0), ("tout", 0), ("part", 1), ("rA", 0, 0, 1), ("tout", 1), ("ryB", 4), ("rA", 1, 0, 2), ("gA", 1, 1, 1),
    ("ryB", 3), ("tout", 2), ("gyB", -2), ("rA", 0, 1, 2), ("tout", 3), ("gB", 1, 3), ("tout", 4), ("gyB", 2),
    ("gA", 0, 1, 1), ("gB", 0, 3), ("fl",), ("ryB", -3), ("rA", 1, 1, 1), ("rB", 0, 1), ("rA", 0, 0, 2), ("part", 2),
    ("rB", 1, 1), ("part", 3), ("gA", 0, 1, 2), ("gA", 1, 1, 2), ("gyB", -1), ("rA", 1, 1, 2), ("gA", 1, 0, 2),
    ("gA", 0, 0, 2), ("fx",), ("gyB", 3), ("pair", 2), ("rB", 0, 2), ("ryB", -2), ("ryB", 2), ("pair", 0),
    ("gA", 1, 1, 3), ("rA", 1, 1, 3), ("gA", 1, 0, 3), ("rA", 0, 1, 3), ("fy",), ("gA", 0, 0, 3), ("gyB", 1),
    ("gA", 0, 1, 3), ("gB", 1, 4), ("rB", 1, 2), ("rA", 0, 0, 3), ("pair", -1), ("rA", 1, 1, 4), ("pair", 3),
    ("gA", 1, 1, 4), ("rA", 0, 1, 4), ("ryB", 1), ("ryB", -1), ("fz",), ("rA", 1, 0, 3), ("gyB", -3), ("pair", 1),
    ("pair", -2), ("gA", 0, 0, 4), ("rB", 1, 3), ("rB", 0, 3), ("gyB", 4), ("rA", 0, 0, 4), ("rA", 1, 0, 4), ("ryA",),
    ("ryB", 0), ("pair", -3), ("rB", 1, 4), ("rB", 0, 4), ("pair", 4), ("fin", 0), ("fin", 1), ("ft",), ("fin", 2),
    ("endA",), ("fin", 3), ("endB",),
)

GROUPS = ((4, 3), (-3, 2), (-2, 1), (-1, 0))


def kernel(
    hid_h, gain_h, w_h, cot_h, fg_h, fm_h, fl_h,
    keys_o, gi_o, gw_o, ng_o, nm_o, nl_o,
    w, hid, nrm, nsib, upper, part, gain, cot, cot_t, kacc, iacc, scl,
    fg, fm, fl, fx, fs, ftot,
    r_a, st_a, yb_s, yb_r, r_b, st_b, ya_s, ya_r,
    ssem, rsem, lsem, in_sem, out_sem, far_sem,
):
    island = lax.axis_index("island")
    f = lax.axis_index("fsdp")
    c = lax.rem(f, 2)
    z = lax.rem(lax.div(f, 2), NZ)
    y = lax.div(f, 2 * NZ)
    x = lax.rem(island, 4)
    yh = lax.div(island, 4)

    def fsdp_of(yy, zz, cc):
        return (yy * NZ + zz) * 2 + cc

    def q_of(dy, dz):
        yy = y if dy == 0 else 1 - y
        return yy * NZ + lax.rem(z + (dz + NZ), NZ)

    zdev = [
        (island, fsdp_of(y, lax.rem(z + 1, NZ), c)),
        (island, fsdp_of(y, lax.rem(z + NZ - 1, NZ), c)),
    ]
    ydev = (island, fsdp_of(1 - y, z, c))
    sdev = (island, fsdp_of(y, z, 1 - c))
    xdev = {j: (yh * 4 + lax.rem(x + j, 4), f) for j in (1, 2, 3)}
    hdev = ((1 - yh) * 4 + x, fsdp_of(1 - y, z, c))
    near = zdev + [ydev, sdev]
    far = [hdev] + [xdev[j] for j in (1, 2, 3)]
    dist = jnp.where(z > 4, NZ - z, z)
    inner = (island, fsdp_of(y, jnp.where(z > 4, lax.rem(z + 1, NZ), lax.rem(z + NZ - 1, NZ)), c))
    outer_z = jnp.where(z > 4, z - 1, lax.rem(z + 1, NZ))
    outermost = (z == 4) | (z == 5)
    outer = (island, fsdp_of(y, outer_z, c))

    def signal(sem, dev):
        pl.semaphore_signal(sem, inc=1, device_id=dev, device_id_type=MESH)

    barrier = pltpu.get_barrier_semaphore()
    for dev in near:
        signal(barrier, dev)

    @pl.when(z == 0)
    def _():
        for dev in far:
            signal(barrier, dev)

    sent = [0, 0]

    def send(name, src, dst, dev):
        group = 0 if name[0] in ("own", "gA", "gB", "gyA", "gyB", "sA", "sB") else 1
        pltpu.make_async_remote_copy(
            src_ref=src, dst_ref=dst, send_sem=ssem.at[group], recv_sem=rsem.at[ARRIVALS[arrival(name)]],
            device_id=dev, device_id_type=MESH,
        ).start()
        sent[group] += math.prod(src.shape) * src.dtype.itemsize

    def arrive(name, ref, dev):
        pltpu.make_async_remote_copy(
            src_ref=ref, dst_ref=ref, send_sem=ssem.at[0], recv_sem=rsem.at[ARRIVALS[name]],
            device_id=dev, device_id_type=MESH,
        ).wait_recv()

    loads = [
        (w_h.at[0], w.at[pl.ds(pl.multiple_of((y * NZ + z) * 512 + c * 256, 256), 256)]),
        (cot_h.at[0], cot.at[0]),
        (fl_h.at[0], fl),
        (gain_h, gain),
        (hid_h.at[0, pl.ds(0, 128)], hid.at[pl.ds(0, 128)]),
        (hid_h.at[0, pl.ds(128, 128)], hid.at[pl.ds(128, 128)]),
        (fg_h, fg),
        (fm_h, fm),
    ]
    local = [pltpu.make_async_copy(s, t, lsem.at[i]) for i, (s, t) in enumerate(loads)]
    for copy in local:
        copy.start()

    @pl.when(z == 0)
    def _():
        pl.semaphore_wait(barrier, len(near) + len(far))

    @pl.when(z != 0)
    def _():
        pl.semaphore_wait(barrier, len(near))

    def wrows(dy, dz, start, size, core=None):
        core = c if core is None else core
        row = q_of(dy, dz) * 512 + core * 256 + start
        return w.at[pl.ds(pl.multiple_of(row, 16), size)]

    def b_span(d, k):
        if k < 4:
            return HALF, 256 - HALF
        half = (256 - HALF) // 32 * 16
        first = 256 - HALF - half
        return (HALF, first) if d == 0 else (HALF + first, half)

    def g_send_a(d, dy, k):
        part_ = wrows(dy, norm_dz(-SIGNS[d] * (k - 1)), 0, HALF)
        send(("gA", d, dy, k), part_, part_, zdev[d])

    def g_send_b(d, k):
        start, size = b_span(d, k)
        part_ = wrows(0, norm_dz(-SIGNS[d] * (k - 1)), start, size)
        send(("gB", d, k), part_, part_, zdev[d])

    def g_send_yb(dz):
        part_ = wrows(0, dz, HALF, 256 - HALF)
        send(("gyB", dz), part_, part_, ydev)

    def to_sibling(which, dy, dz):
        start, size = (0, HALF) if which == "sA" else (HALF, 256 - HALF)
        part_ = wrows(dy, dz, start, size)
        send((which, dy, dz), part_, part_, sdev)

    def step_start():
        for i in range(2):
            local[i].wait()
        send(("gyA",), wrows(0, 0, 0, HALF), wrows(0, 0, 0, HALF), ydev)
        for d in (0, 1):
            g_send_b(d, 1)
        g_send_yb(0)
        for d in (0, 1):
            g_send_a(d, 0, 1)
        send(("own",), wrows(0, 0, 0, 256), wrows(0, 0, 0, 256), sdev)
        send(("cot",), cot.at[0], cot.at[1], sdev)
        local[2].wait()
        kacc[...] = jnp.zeros_like(kacc)
        iacc[...] = jnp.zeros_like(iacc)
        cot_t[0] = cot[0].T

    def step_gya():
        arrive(("gyA",), wrows(1, 0, 0, HALF), ydev)
        for d in (0, 1):
            g_send_a(d, 1, 1)
        to_sibling("sA", 1, 0)

    def step_ga(d, dy, k):
        dz = norm_dz(-SIGNS[d] * k)
        arrive(("gA", d, dy, k), wrows(dy, dz, 0, HALF), zdev[d])
        if k < chain_len(d, dy):
            g_send_a(d, dy, k + 1)
        to_sibling("sA", dy, dz)

    def step_gb(d, k):
        dz = norm_dz(-SIGNS[d] * k)
        if k == 4:
            arrive(("gB", 4), wrows(0, dz, HALF, 256 - HALF), zdev[d])
        else:
            arrive(("gB", d, k), wrows(0, dz, HALF, 256 - HALF), zdev[d])
            g_send_b(d, k + 1)
        g_send_yb(dz)
        to_sibling("sB", 0, dz)

    def step_gyb(dz):
        arrive(("gyB", dz), wrows(1, dz, HALF, 256 - HALF), ydev)
        to_sibling("sB", 1, dz)

    def norm_block(i, carry):
        rows = pl.ds(pl.multiple_of(i * 32, 32), 32)
        acc = jnp.zeros((32, 512), F32)
        for j in range(16):
            h = hid[rows, j * 512:(j + 1) * 512].astype(F32)
            acc = acc + h * h
        total = jnp.sum(acc, axis=-1, keepdims=True)
        s = lax.rsqrt(total / D + epsilon)
        scl[rows, :] = s
        for j in range(16):
            h = hid[rows, j * 512:(j + 1) * 512].astype(F32)
            g = gain[:, j * 512:(j + 1) * 512].astype(F32)
            n = (h * s * g).astype(BF16)
            nrm[0, rows, j * 256:(j + 1) * 256] = n[:, :256]
            nrm[1, rows, j * 256:(j + 1) * 256] = n[:, 256:]
        return carry

    def step_norm(i):
        if i == 0:
            local[3].wait()
        local[4 + i].wait()
        lax.fori_loop(i * 4, i * 4 + 4, norm_block, 0)
        rows = pl.ds(i * 128, 128)
        send(("n", i), nrm.at[1 - c, rows], nsib.at[rows], sdev)

    def step_part(p):
        if p == 0:
            arrive(("n",), w.at[pl.ds(0, 2304)], sdev)
            cot_t[1] = cot[1].T
        first, second = GROUPS[p]

        def one(i, carry):
            zz = lax.rem(z + NZ + first + (second - first) * lax.div(i, 2), NZ)
            q = lax.rem(y + lax.rem(i, 2), 2) * NZ + zz
            cols = pl.ds(pl.multiple_of(q * 256, 256), 256)
            a = jnp.dot(cot_t[0], nrm[c, :, cols], preferred_element_type=F32)
            b = jnp.dot(cot_t[1], nsib[:, cols], preferred_element_type=F32)
            part[q] = a + b
            return carry

        lax.fori_loop(0, 4, one, 0)

    def work_on(q):
        cols = pl.ds(pl.multiple_of(q * 512, 512), 512)
        half = pl.ds(pl.multiple_of(q * 256, 256), 256)
        rows = pl.multiple_of(q * 512, 512)
        w0 = w[pl.ds(rows, 256), :]
        w1 = w[pl.ds(rows + 256, 256), :]
        kacc[...] += jnp.dot(nrm[0, :, half], w0, preferred_element_type=F32) + jnp.dot(
            nrm[1, :, half], w1, preferred_element_type=F32
        )
        back = lax.dot_general(
            cot[0], w[pl.ds(rows, 512), :], (((1,), (1,)), ((), ())), preferred_element_type=F32
        )
        u = back * gain[:, cols].astype(F32)
        upper[:, cols] = u
        t = u * hid[:, cols].astype(F32)
        iacc[...] += (t[:, :128] + t[:, 128:256]) + (t[:, 256:384] + t[:, 384:])

    def step_pair(dz):
        arrive(("s", dz), w.at[pl.ds(pl.multiple_of(q_of(0, dz) * 512, 512), 512)], sdev)

        def one(i, carry):
            work_on(lax.rem(y + i, 2) * NZ + lax.rem(z + NZ + dz, NZ))
            return carry

        lax.fori_loop(0, 2, one, 0)

    def add_into(dst, terms, rows):
        def some(r):
            total = terms[0][r, :].astype(F32)
            for term in terms[1:]:
                total = total + term[r, :].astype(F32)
            dst[r, :] = total.astype(dst.dtype)

        def one(i, carry):
            some(pl.ds(pl.multiple_of(i * 64, 64), 64))
            return carry

        lax.fori_loop(0, rows // 64, one, 0)
        if rows % 64:
            some(pl.ds(rows // 64 * 64, rows % 64))

    def p_rows(dy, dz, start, size):
        return part.at[q_of(dy, dz), pl.ds(start, size)]

    def step_ryb(dz):
        slot = dz + 3
        add_into(yb_s.at[slot], [p_rows(1, dz, RA, RB)], RB)
        send(("ryB", dz), yb_s.at[slot], yb_r.at[slot], ydev)

    def step_ra(d, dy, t):
        dz = norm_dz(SIGNS[d] * (5 - t))
        mine = p_rows(dy, dz, 0, RA)
        if t == 5 - chain_len(d, dy):
            buf = st_a.at[d, dy]
            add_into(buf, [mine], RA)
        else:
            buf = r_a.at[d, dy, t - 2]
            arrive(("rA", d, dy, t - 1), buf, zdev[d])
            add_into(buf, [buf, mine], RA)
        send(("rA", d, dy, t), buf, r_a.at[d, dy, t - 1], zdev[d])

    def arrive_yb(dz):
        arrive(("ryB", dz), yb_r.at[dz + 3], ydev)

    def step_rb(d, t):
        dz = norm_dz(SIGNS[d] * (5 - t))
        slot = dz + 3
        spans = ((0, RB0), (RB0, RB - RB0))
        start, size = spans[d]
        span = pl.ds(start, size)
        if t == 1:
            if not seen:
                arrive_yb(dz)
                seen.append(dz)
            buf = st_b.at[d, pl.ds(0, size)]
            add_into(buf, [p_rows(0, dz, RA + start, size), yb_r.at[slot, span]], size)
            send(("rB", d, 1), buf, r_b.at[d, 0, span], zdev[d])
            return
        arrive_yb(dz)
        buf = r_b.at[d, t - 2]
        if t == 2:
            arrive(("rB", d, 1), buf.at[span], zdev[d])
            add_into(buf.at[span], [buf.at[span], p_rows(0, dz, RA + start, size), yb_r.at[slot, span]], size)
            start, size = spans[1 - d]
            span = pl.ds(start, size)
            add_into(buf.at[span], [p_rows(0, dz, RA + start, size), yb_r.at[slot, span]], size)
        else:
            arrive(("rB", d, t - 1), buf, zdev[d])
            add_into(buf, [buf, p_rows(0, dz, RA, RB), yb_r.at[slot]], RB)
        send(("rB", d, t), buf, r_b.at[d, t - 1], zdev[d])

    seen = []

    def last_a(dy):
        arrive(("rA", 4, dy), w.at[pl.ds(0, RA)], zdev[0])
        return [p_rows(dy, 0, 0, RA), r_a.at[0, dy, 3], r_a.at[1, dy, 3]]

    ended = []

    def write_gw(block, terms, start, size):
        mine = part.at[q_of(0, 0)]
        add_into(mine.at[pl.ds(start, size)], terms, size)
        blocks = (0,) if block == 0 else (2, 3)
        for i in blocks + ((1,) if ended else ()):
            gw_o[0, :, i * 128:(i + 1) * 128] = mine[pl.ds(i * 128, 128), :].T
        ended.append(block)

    def step_rya():
        add_into(ya_s, last_a(1), RA)
        send(("ryA",), ya_s, ya_r, ydev)

    def step_end_b():
        arrive_yb(0)
        arrive(("rB", 4), w.at[pl.ds(0, RB)], zdev[0])
        write_gw(2, [p_rows(0, 0, RA, RB), yb_r.at[3], r_b.at[0, 3], r_b.at[1, 3]], RA, RB)

    def step_end_a():
        terms = last_a(0)
        arrive(("ryA",), ya_r, ydev)
        write_gw(0, terms + [ya_r], 0, RA)

    mine64 = pl.ds(pl.multiple_of(x * 64, 64), 64)

    def step_tin(i):
        @pl.when(dist == 4 - i)
        def _():
            pl.when(jnp.logical_not(outermost))(lambda: pl.semaphore_wait(in_sem, 1))
            signal(in_sem, inner)

    def step_far():
        @pl.when(z == 0)
        def _():
            pl.semaphore_wait(in_sem, 2)
            for dev in far:
                signal(far_sem, dev)

    def step_tout(i):
        @pl.when(dist == i)
        def _():
            if i == 0:
                pl.semaphore_wait(far_sem, len(far))
                for dev in zdev:
                    signal(out_sem, dev)
            else:
                pl.semaphore_wait(out_sem, 1)
                pl.when(jnp.logical_not(outermost))(lambda: signal(out_sem, outer))

    def step_fl():
        for j in (1, 2, 3):
            quarter = pl.ds(pl.multiple_of(lax.rem(x + j, 4) * 64, 64), 64)
            send(("fx", j), fl.at[quarter], fx.at[j - 1], xdev[j])

    def step_fx():
        arrive(("fx",), w.at[pl.ds(0, 192)], xdev[1])
        others = [fx[j].astype(F32) for j in range(3)]
        fs[0] = (fl[mine64, :].astype(F32) + others[1]) + (others[0] + others[2])
        send(("fy",), fs.at[0], fs.at[1], ydev)

    def step_fy():
        arrive(("fy",), fs.at[1], ydev)
        send(("fz",), fs.at[1], fs.at[2], hdev)

    def step_fz():
        arrive(("fz",), fs.at[2], hdev)
        ftot[mine64, :] = (fs[0] + fs[2]) / ISLANDS
        for j in (1, 2, 3):
            send(("ft", j), ftot.at[mine64], ftot.at[mine64], xdev[j])

    def step_ft():
        arrive(("ft",), ftot.at[pl.ds(0, 192)], xdev[1])
        local[6].wait()
        local[7].wait()

        def outer_step(i, carry):
            r = pl.ds(pl.multiple_of(i * 32, 32), 32)
            g = fg[r, :]
            pseudo = g - ftot[r, :]
            moment = outer_momentum * fm[r, :] + pseudo
            new = g - outer_rate * (pseudo + outer_momentum * moment)
            nm_o[r, :] = moment
            ng_o[r, :] = new
            nl_o[0, r, :] = (mix_weight * fl[r, :].astype(F32) + (1.0 - mix_weight) * new).astype(BF16)
            return carry

        lax.fori_loop(0, 8, outer_step, 0)

    def step_fin(p):
        if p == 0:
            keys_o[0] = kacc[...].astype(BF16)

        def finish(i, carry):
            r = pl.ds(pl.multiple_of(i * 32, 32), 32)
            s = scl[r, :]
            inner = jnp.sum(iacc[r, :], axis=-1, keepdims=True) / D
            coef = s * s * s * inner
            for j in range(16):
                cols = slice(j * 512, (j + 1) * 512)
                gi_o[0, r, cols] = (s * upper[r, cols] - hid[r, cols].astype(F32) * coef).astype(BF16)
            return carry

        lax.fori_loop(2 * p, 2 * p + 2, finish, 0)

    steps = {
        "start": step_start, "gyA": step_gya, "gA": step_ga, "gB": step_gb, "gyB": step_gyb,
        "norm": step_norm, "part": step_part, "ryB": step_ryb, "rA": step_ra, "rB": step_rb,
        "tin": step_tin, "far": step_far, "tout": step_tout, "fl": step_fl, "fx": step_fx, "fy": step_fy, "fz": step_fz, "ft": step_ft, "pair": step_pair, "fin": step_fin,
        "ryA": step_rya, "endB": step_end_b, "endA": step_end_a,
    }
    for step in ORDER:
        steps[step[0]](*step[1:])

    for group in (0, 1):
        everything = w.at[pl.ds(0, sent[group] // (KC * 2))]
        pltpu.make_async_remote_copy(
            src_ref=everything, dst_ref=everything, send_sem=ssem.at[group], recv_sem=rsem.at[0],
            device_id=sdev, device_id_type=MESH,
        ).wait_send()


def store(*refs):
    n = (len(refs) - 1) // 2
    copies = [pltpu.make_async_copy(refs[i], refs[n + i], refs[-1].at[i]) for i in range(n)]
    for copy in copies:
        copy.start()
    for copy in copies:
        copy.wait()


def body(*args):
    outs = [
        ((1, TOK, KC), BF16),
        ((1, TOK, D), BF16),
        ((1, TOK, KC), F32),
        ((TOK, KC), F32),
        ((TOK, KC), F32),
        ((1, TOK, KC), BF16),
    ]
    vm = pltpu.VMEM
    results = pl.pallas_call(
        kernel,
        out_shape=[vm(*o) for o in outs],
        in_specs=[pl.BlockSpec(memory_space=pltpu.HBM)] * 7,
        out_specs=[pl.BlockSpec(memory_space=vm)] * 6,
        scratch_shapes=[
            vm((D, KC), BF16),
            vm((TOK, D), BF16),
            vm((2, TOK, D // 2), BF16),
            vm((TOK, D // 2), BF16),
            vm((TOK, D), F32),
            vm((NCHIP, KC, 256), F32),
            vm((1, D), BF16),
            vm((2, TOK, KC), BF16),
            vm((2, KC, TOK), BF16),
            vm((TOK, KC), F32),
            vm((TOK, 128), F32),
            vm((TOK, 1), F32),
            vm((TOK, KC), F32),
            vm((TOK, KC), F32),
            vm((TOK, KC), BF16),
            vm((3, 64, KC), BF16),
            vm((3, 64, KC), F32),
            vm((TOK, KC), F32),
            vm((2, 2, 4, RA, 256), BF16),
            vm((2, 2, RA, 256), BF16),
            vm((8, RB, 256), BF16),
            vm((8, RB, 256), BF16),
            vm((2, 4, RB, 256), BF16),
            vm((2, RB0, 256), BF16),
            vm((RA, 256), BF16),
            vm((RA, 256), BF16),
            pltpu.SemaphoreType.DMA((2,)),
            pltpu.SemaphoreType.DMA((len(ARRIVALS),)),
            pltpu.SemaphoreType.DMA((8,)),
            pltpu.SemaphoreType.REGULAR,
            pltpu.SemaphoreType.REGULAR,
            pltpu.SemaphoreType.REGULAR,
        ],
        compiler_params=pltpu.CompilerParams(
            collective_id=0, has_side_effects=True, vmem_limit_bytes=56 * 2**20
        ),
    )(*args)
    return tuple(
        pl.pallas_call(
            store,
            out_shape=[jax.ShapeDtypeStruct(*o) for o in outs],
            in_specs=[pl.BlockSpec(memory_space=pl.ANY)] * 6,
            out_specs=[pl.BlockSpec(memory_space=pl.ANY)] * 6,
            scratch_shapes=[pltpu.SemaphoreType.DMA((6,))],
            compiler_params=pltpu.CompilerParams(vmem_limit_bytes=2**20),
        )(*results)
    )


def solution(mesh):
    rows = P("island", "fsdp", None)
    frag = P("fsdp", None)
    return jax.shard_map(
        body,
        mesh=mesh,
        in_specs=(rows, P("island", None), rows, rows, frag, frag, rows),
        out_specs=(rows, rows, rows, frag, frag, rows),
        check_vma=False,
    )
```

```python
import math

import jax
import jax.numpy as jnp
from jax import lax
from jax.experimental import pallas as pl
from jax.experimental.pallas import tpu as pltpu
from jax.sharding import PartitionSpec as P

epsilon = 1e-05
outer_rate = 0.7
outer_momentum = 0.9
mix_weight = 0.5

MESH = pl.DeviceIdType.MESH
F32 = jnp.float32
BF16 = jnp.bfloat16

D = 8192
KC = 512
TOK = 256
NZ = 8
ISLANDS = 8
NCHIP = 16
HALF = 112
RA = 240
RB = KC - RA
RB0 = RB // 32 * 16 + RB % 32
SIGNS = (1, -1)


def norm_dz(dz):
    dz = dz % NZ
    return dz - NZ if dz > 4 else dz


def chain_len(d, dy):
    return 4 if d == dy else 3


def arrival(name):
    kind = name[0]
    if kind in ("own", "sA", "sB"):
        return ("s", name[2] if len(name) > 1 else 0)
    if kind in ("cot", "n"):
        return ("n",)
    if kind in ("fx", "ft"):
        return (kind,)
    if kind in ("gB", "rB") and name[2] == 4:
        return (kind, 4)
    if kind == "rA" and name[3] == 4:
        return (kind, 4, name[2])
    return name


def arrivals():
    names = [("gyA",), ("ryA",), ("n",), ("fx",), ("fy",), ("fz",), ("ft",), ("gB", 4), ("rB", 4)]
    for dy in (0, 1):
        names += [("rA", 4, dy)]
        for d in (0, 1):
            names += [("gA", d, dy, k) for k in range(1, 1 + chain_len(d, dy))]
            names += [("rA", d, dy, t) for t in range(5 - chain_len(d, dy), 4)]
    for k in (1, 2, 3):
        names += [(kind, d, k) for kind in ("gB", "rB") for d in (0, 1)]
    for dz in range(-3, 5):
        names += [(kind, dz) for kind in ("gyB", "ryB", "s")]
    return {name: i for i, name in enumerate(names)}


ARRIVALS = arrivals()

ORDER = (
    ("start",), ("norm", 0), ("tin", 0), ("norm", 1), ("tin", 1), ("gB", 0, 1), ("gB", 1, 1), ("tin", 2),
    ("gA", 1, 0, 1), ("tin", 3), ("gyB", 0), ("gyA",), ("gA", 0, 0, 1), ("far",), ("gB", 0, 2), ("gB", 1, 2),
    ("part", 0), ("tout", 0), ("part", 1), ("rA", 0, 0, 1), ("tout", 1), ("ryB", 4), ("rA", 1, 0, 2), ("gA", 1, 1, 1),
    ("ryB", 3), ("tout", 2), ("gyB", -2), ("rA", 0, 1, 2), ("tout", 3), ("gB", 1, 3), ("tout", 4), ("gyB", 2),
    ("gA", 0, 1, 1), ("gB", 0, 3), ("fl",), ("ryB", -3), ("rA", 1, 1, 1), ("rB", 0, 1), ("rA", 0, 0, 2), ("part", 2),
    ("rB", 1, 1), ("part", 3), ("gA", 0, 1, 2), ("gA", 1, 1, 2), ("gyB", -1), ("rA", 1, 1, 2), ("gA", 1, 0, 2),
    ("gA", 0, 0, 2), ("fx",), ("gyB", 3), ("pair", 2), ("rB", 0, 2), ("ryB", -2), ("ryB", 2), ("pair", 0),
    ("gA", 1, 1, 3), ("rA", 1, 1, 3), ("gA", 1, 0, 3), ("rA", 0, 1, 3), ("fy",), ("gA", 0, 0, 3), ("gyB", 1),
    ("gA", 0, 1, 3), ("gB", 1, 4), ("rB", 1, 2), ("rA", 0, 0, 3), ("pair", -1), ("rA", 1, 1, 4), ("pair", 3),
    ("gA", 1, 1, 4), ("rA", 0, 1, 4), ("ryB", 1), ("ryB", -1), ("fz",), ("rA", 1, 0, 3), ("gyB", -3), ("pair", 1),
    ("pair", -2), ("gA", 0, 0, 4), ("rB", 1, 3), ("rB", 0, 3), ("gyB", 4), ("rA", 0, 0, 4), ("rA", 1, 0, 4), ("ryA",),
    ("ryB", 0), ("pair", -3), ("rB", 1, 4), ("rB", 0, 4), ("pair", 4), ("fin", 0), ("fin", 1), ("ft",), ("fin", 2),
    ("endA",), ("fin", 3), ("endB",),
)

GROUPS = ((4, 3), (-3, 2), (-2, 1), (-1, 0))


def kernel(
    hid_h, gain_h, w_h, cot_h, fg_h, fm_h, fl_h,
    keys_o, gi_o, gw_o, ng_o, nm_o, nl_o,
    w, hid, nrm, nsib, upper, part, gain, cot, cot_t, kacc, iacc, scl,
    fg, fm, fl, fx, fs, ftot,
    r_a, st_a, yb_s, yb_r, r_b, st_b, ya_s, ya_r,
    ssem, rsem, lsem, in_sem, out_sem, far_sem,
):
    island = lax.axis_index("island")
    f = lax.axis_index("fsdp")
    c = lax.rem(f, 2)
    z = lax.rem(lax.div(f, 2), NZ)
    y = lax.div(f, 2 * NZ)
    x = lax.rem(island, 4)
    yh = lax.div(island, 4)

    def fsdp_of(yy, zz, cc):
        return (yy * NZ + zz) * 2 + cc

    def q_of(dy, dz):
        yy = y if dy == 0 else 1 - y
        return yy * NZ + lax.rem(z + (dz + NZ), NZ)

    zdev = [
        (island, fsdp_of(y, lax.rem(z + 1, NZ), c)),
        (island, fsdp_of(y, lax.rem(z + NZ - 1, NZ), c)),
    ]
    ydev = (island, fsdp_of(1 - y, z, c))
    sdev = (island, fsdp_of(y, z, 1 - c))
    xdev = {j: (yh * 4 + lax.rem(x + j, 4), f) for j in (1, 2, 3)}
    hdev = ((1 - yh) * 4 + x, fsdp_of(1 - y, z, c))
    near = zdev + [ydev, sdev]
    far = [hdev] + [xdev[j] for j in (1, 2, 3)]
    dist = jnp.where(z > 4, NZ - z, z)
    inner = (island, fsdp_of(y, jnp.where(z > 4, lax.rem(z + 1, NZ), lax.rem(z + NZ - 1, NZ)), c))
    outer_z = jnp.where(z > 4, z - 1, lax.rem(z + 1, NZ))
    outermost = (z == 4) | (z == 5)
    outer = (island, fsdp_of(y, outer_z, c))

    def signal(sem, dev):
        pl.semaphore_signal(sem, inc=1, device_id=dev, device_id_type=MESH)

    barrier = pltpu.get_barrier_semaphore()
    for dev in near:
        signal(barrier, dev)

    @pl.when(z == 0)
    def _():
        for dev in far:
            signal(barrier, dev)

    sent = [0, 0]

    def send(name, src, dst, dev):
        group = 0 if name[0] in ("own", "gA", "gB", "gyA", "gyB", "sA", "sB") else 1
        pltpu.make_async_remote_copy(
            src_ref=src, dst_ref=dst, send_sem=ssem.at[group], recv_sem=rsem.at[ARRIVALS[arrival(name)]],
            device_id=dev, device_id_type=MESH,
        ).start()
        sent[group] += math.prod(src.shape) * src.dtype.itemsize

    def arrive(name, ref, dev):
        pltpu.make_async_remote_copy(
            src_ref=ref, dst_ref=ref, send_sem=ssem.at[0], recv_sem=rsem.at[ARRIVALS[name]],
            device_id=dev, device_id_type=MESH,
        ).wait_recv()

    loads = [
        (w_h.at[0], w.at[pl.ds(pl.multiple_of((y * NZ + z) * 512 + c * 256, 256), 256)]),
        (cot_h.at[0], cot.at[0]),
        (fl_h.at[0], fl),
        (gain_h, gain),
        (hid_h.at[0, pl.ds(0, 128)], hid.at[pl.ds(0, 128)]),
        (hid_h.at[0, pl.ds(128, 128)], hid.at[pl.ds(128, 128)]),
        (fg_h, fg),
        (fm_h, fm),
    ]
    local = [pltpu.make_async_copy(s, t, lsem.at[i]) for i, (s, t) in enumerate(loads)]
    for copy in local:
        copy.start()

    @pl.when(z == 0)
    def _():
        pl.semaphore_wait(barrier, len(near) + len(far))

    @pl.when(z != 0)
    def _():
        pl.semaphore_wait(barrier, len(near))

    def wrows(dy, dz, start, size, core=None):
        core = c if core is None else core
        row = q_of(dy, dz) * 512 + core * 256 + start
        return w.at[pl.ds(pl.multiple_of(row, 16), size)]

    def b_span(d, k):
        if k < 4:
            return HALF, 256 - HALF
        half = (256 - HALF) // 32 * 16
        first = 256 - HALF - half
        return (HALF, first) if d == 0 else (HALF + first, half)

    def g_send_a(d, dy, k):
        part_ = wrows(dy, norm_dz(-SIGNS[d] * (k - 1)), 0, HALF)
        send(("gA", d, dy, k), part_, part_, zdev[d])

    def g_send_b(d, k):
        start, size = b_span(d, k)
        part_ = wrows(0, norm_dz(-SIGNS[d] * (k - 1)), start, size)
        send(("gB", d, k), part_, part_, zdev[d])

    def g_send_yb(dz):
        part_ = wrows(0, dz, HALF, 256 - HALF)
        send(("gyB", dz), part_, part_, ydev)

    def to_sibling(which, dy, dz):
        start, size = (0, HALF) if which == "sA" else (HALF, 256 - HALF)
        part_ = wrows(dy, dz, start, size)
        send((which, dy, dz), part_, part_, sdev)

    def step_start():
        def own(name, start, size, dev):
            send(name, w_h.at[0, pl.ds(start, size)], wrows(0, 0, start, size), dev)

        for d in (0, 1):
            own(("gB", d, 1), HALF, 256 - HALF, zdev[d])
        own(("gyA",), 0, HALF, ydev)
        own(("gyB", 0), HALF, 256 - HALF, ydev)
        for d in (0, 1):
            own(("gA", d, 0, 1), 0, HALF, zdev[d])
        own(("own",), 0, 256, sdev)
        send(("cot",), cot_h.at[0], cot.at[1], sdev)
        for i in range(3):
            local[i].wait()
        kacc[...] = jnp.zeros_like(kacc)
        iacc[...] = jnp.zeros_like(iacc)
        cot_t[0] = cot[0].T

    def step_gya():
        arrive(("gyA",), wrows(1, 0, 0, HALF), ydev)
        for d in (0, 1):
            g_send_a(d, 1, 1)
        to_sibling("sA", 1, 0)

    def step_ga(d, dy, k):
        dz = norm_dz(-SIGNS[d] * k)
        arrive(("gA", d, dy, k), wrows(dy, dz, 0, HALF), zdev[d])
        if k < chain_len(d, dy):
            g_send_a(d, dy, k + 1)
        to_sibling("sA", dy, dz)

    def step_gb(d, k):
        dz = norm_dz(-SIGNS[d] * k)
        if k == 4:
            arrive(("gB", 4), wrows(0, dz, HALF, 256 - HALF), zdev[d])
        else:
            arrive(("gB", d, k), wrows(0, dz, HALF, 256 - HALF), zdev[d])
            g_send_b(d, k + 1)
        g_send_yb(dz)
        to_sibling("sB", 0, dz)

    def step_gyb(dz):
        arrive(("gyB", dz), wrows(1, dz, HALF, 256 - HALF), ydev)
        to_sibling("sB", 1, dz)

    def norm_block(i, carry):
        rows = pl.ds(pl.multiple_of(i * 32, 32), 32)
        acc = jnp.zeros((32, 512), F32)
        for j in range(16):
            h = hid[rows, j * 512:(j + 1) * 512].astype(F32)
            acc = acc + h * h
        total = jnp.sum(acc, axis=-1, keepdims=True)
        s = lax.rsqrt(total / D + epsilon)
        scl[rows, :] = s
        for j in range(16):
            h = hid[rows, j * 512:(j + 1) * 512].astype(F32)
            g = gain[:, j * 512:(j + 1) * 512].astype(F32)
            n = (h * s * g).astype(BF16)
            nrm[0, rows, j * 256:(j + 1) * 256] = n[:, :256]
            nrm[1, rows, j * 256:(j + 1) * 256] = n[:, 256:]
        return carry

    def step_norm(i):
        if i == 0:
            local[3].wait()
        local[4 + i].wait()
        lax.fori_loop(i * 4, i * 4 + 4, norm_block, 0)
        rows = pl.ds(i * 128, 128)
        send(("n", i), nrm.at[1 - c, rows], nsib.at[rows], sdev)

    def step_part(p):
        if p == 0:
            arrive(("n",), w.at[pl.ds(0, 2304)], sdev)
            cot_t[1] = cot[1].T
        first, second = GROUPS[p]

        def one(i, carry):
            zz = lax.rem(z + NZ + first + (second - first) * lax.div(i, 2), NZ)
            q = lax.rem(y + lax.rem(i, 2), 2) * NZ + zz
            cols = pl.ds(pl.multiple_of(q * 256, 256), 256)
            a = jnp.dot(cot_t[0], nrm[c, :, cols], preferred_element_type=F32)
            b = jnp.dot(cot_t[1], nsib[:, cols], preferred_element_type=F32)
            part[q] = a + b
            return carry

        lax.fori_loop(0, 4, one, 0)

    def work_on(q):
        cols = pl.ds(pl.multiple_of(q * 512, 512), 512)
        half = pl.ds(pl.multiple_of(q * 256, 256), 256)
        rows = pl.multiple_of(q * 512, 512)
        w0 = w[pl.ds(rows, 256), :]
        w1 = w[pl.ds(rows + 256, 256), :]
        kacc[...] += jnp.dot(nrm[0, :, half], w0, preferred_element_type=F32) + jnp.dot(
            nrm[1, :, half], w1, preferred_element_type=F32
        )
        back = lax.dot_general(
            cot[0], w[pl.ds(rows, 512), :], (((1,), (1,)), ((), ())), preferred_element_type=F32
        )
        u = back * gain[:, cols].astype(F32)
        upper[:, cols] = u
        t = u * hid[:, cols].astype(F32)
        iacc[...] += (t[:, :128] + t[:, 128:256]) + (t[:, 256:384] + t[:, 384:])

    def step_pair(dz):
        arrive(("s", dz), w.at[pl.ds(pl.multiple_of(q_of(0, dz) * 512, 512), 512)], sdev)

        def one(i, carry):
            work_on(lax.rem(y + i, 2) * NZ + lax.rem(z + NZ + dz, NZ))
            return carry

        lax.fori_loop(0, 2, one, 0)

    def add_into(dst, terms, rows):
        def some(r):
            total = terms[0][r, :].astype(F32)
            for term in terms[1:]:
                total = total + term[r, :].astype(F32)
            dst[r, :] = total.astype(dst.dtype)

        def one(i, carry):
            some(pl.ds(pl.multiple_of(i * 64, 64), 64))
            return carry

        lax.fori_loop(0, rows // 64, one, 0)
        if rows % 64:
            some(pl.ds(rows // 64 * 64, rows % 64))

    def p_rows(dy, dz, start, size):
        return part.at[q_of(dy, dz), pl.ds(start, size)]

    def step_ryb(dz):
        slot = dz + 3
        add_into(yb_s.at[slot], [p_rows(1, dz, RA, RB)], RB)
        send(("ryB", dz), yb_s.at[slot], yb_r.at[slot], ydev)

    def step_ra(d, dy, t):
        dz = norm_dz(SIGNS[d] * (5 - t))
        mine = p_rows(dy, dz, 0, RA)
        if t == 5 - chain_len(d, dy):
            buf = st_a.at[d, dy]
            add_into(buf, [mine], RA)
        else:
            buf = r_a.at[d, dy, t - 2]
            arrive(("rA", d, dy, t - 1), buf, zdev[d])
            add_into(buf, [buf, mine], RA)
        send(("rA", d, dy, t), buf, r_a.at[d, dy, t - 1], zdev[d])

    def arrive_yb(dz):
        arrive(("ryB", dz), yb_r.at[dz + 3], ydev)

    def step_rb(d, t):
        dz = norm_dz(SIGNS[d] * (5 - t))
        slot = dz + 3
        spans = ((0, RB0), (RB0, RB - RB0))
        start, size = spans[d]
        span = pl.ds(start, size)
        if t == 1:
            if not seen:
                arrive_yb(dz)
                seen.append(dz)
            buf = st_b.at[d, pl.ds(0, size)]
            add_into(buf, [p_rows(0, dz, RA + start, size), yb_r.at[slot, span]], size)
            send(("rB", d, 1), buf, r_b.at[d, 0, span], zdev[d])
            return
        arrive_yb(dz)
        buf = r_b.at[d, t - 2]
        if t == 2:
            arrive(("rB", d, 1), buf.at[span], zdev[d])
            add_into(buf.at[span], [buf.at[span], p_rows(0, dz, RA + start, size), yb_r.at[slot, span]], size)
            start, size = spans[1 - d]
            span = pl.ds(start, size)
            add_into(buf.at[span], [p_rows(0, dz, RA + start, size), yb_r.at[slot, span]], size)
        else:
            arrive(("rB", d, t - 1), buf, zdev[d])
            add_into(buf, [buf, p_rows(0, dz, RA, RB), yb_r.at[slot]], RB)
        send(("rB", d, t), buf, r_b.at[d, t - 1], zdev[d])

    seen = []

    def last_a(dy):
        arrive(("rA", 4, dy), w.at[pl.ds(0, RA)], zdev[0])
        return [p_rows(dy, 0, 0, RA), r_a.at[0, dy, 3], r_a.at[1, dy, 3]]

    ended = []

    def write_gw(block, terms, start, size):
        mine = part.at[q_of(0, 0)]
        add_into(mine.at[pl.ds(start, size)], terms, size)
        blocks = (0,) if block == 0 else (2, 3)
        for i in blocks + ((1,) if ended else ()):
            gw_o[0, :, i * 128:(i + 1) * 128] = mine[pl.ds(i * 128, 128), :].T
        ended.append(block)

    def step_rya():
        add_into(ya_s, last_a(1), RA)
        send(("ryA",), ya_s, ya_r, ydev)

    def step_end_b():
        arrive_yb(0)
        arrive(("rB", 4), w.at[pl.ds(0, RB)], zdev[0])
        write_gw(2, [p_rows(0, 0, RA, RB), yb_r.at[3], r_b.at[0, 3], r_b.at[1, 3]], RA, RB)

    def step_end_a():
        terms = last_a(0)
        arrive(("ryA",), ya_r, ydev)
        write_gw(0, terms + [ya_r], 0, RA)

    mine64 = pl.ds(pl.multiple_of(x * 64, 64), 64)

    def step_tin(i):
        @pl.when(dist == 4 - i)
        def _():
            pl.when(jnp.logical_not(outermost))(lambda: pl.semaphore_wait(in_sem, 1))
            signal(in_sem, inner)

    def step_far():
        @pl.when(z == 0)
        def _():
            pl.semaphore_wait(in_sem, 2)
            for dev in far:
                signal(far_sem, dev)

    def step_tout(i):
        @pl.when(dist == i)
        def _():
            if i == 0:
                pl.semaphore_wait(far_sem, len(far))
                for dev in zdev:
                    signal(out_sem, dev)
            else:
                pl.semaphore_wait(out_sem, 1)
                pl.when(jnp.logical_not(outermost))(lambda: signal(out_sem, outer))

    def step_fl():
        for j in (1, 2, 3):
            quarter = pl.ds(pl.multiple_of(lax.rem(x + j, 4) * 64, 64), 64)
            send(("fx", j), fl.at[quarter], fx.at[j - 1], xdev[j])

    def step_fx():
        arrive(("fx",), w.at[pl.ds(0, 192)], xdev[1])
        others = [fx[j].astype(F32) for j in range(3)]
        fs[0] = (fl[mine64, :].astype(F32) + others[1]) + (others[0] + others[2])
        send(("fy",), fs.at[0], fs.at[1], ydev)

    def step_fy():
        arrive(("fy",), fs.at[1], ydev)
        send(("fz",), fs.at[1], fs.at[2], hdev)

    def step_fz():
        arrive(("fz",), fs.at[2], hdev)
        ftot[mine64, :] = (fs[0] + fs[2]) / ISLANDS
        for j in (1, 2, 3):
            send(("ft", j), ftot.at[mine64], ftot.at[mine64], xdev[j])

    def step_ft():
        arrive(("ft",), ftot.at[pl.ds(0, 192)], xdev[1])
        local[6].wait()
        local[7].wait()

        def outer_step(i, carry):
            r = pl.ds(pl.multiple_of(i * 32, 32), 32)
            g = fg[r, :]
            pseudo = g - ftot[r, :]
            moment = outer_momentum * fm[r, :] + pseudo
            new = g - outer_rate * (pseudo + outer_momentum * moment)
            nm_o[r, :] = moment
            ng_o[r, :] = new
            nl_o[0, r, :] = (mix_weight * fl[r, :].astype(F32) + (1.0 - mix_weight) * new).astype(BF16)
            return carry

        lax.fori_loop(0, 8, outer_step, 0)

    def step_fin(p):
        if p == 0:
            keys_o[0] = kacc[...].astype(BF16)

        def finish(i, carry):
            r = pl.ds(pl.multiple_of(i * 32, 32), 32)
            s = scl[r, :]
            inner = jnp.sum(iacc[r, :], axis=-1, keepdims=True) / D
            coef = s * s * s * inner
            for j in range(16):
                cols = slice(j * 512, (j + 1) * 512)
                gi_o[0, r, cols] = (s * upper[r, cols] - hid[r, cols].astype(F32) * coef).astype(BF16)
            return carry

        lax.fori_loop(2 * p, 2 * p + 2, finish, 0)

    steps = {
        "start": step_start, "gyA": step_gya, "gA": step_ga, "gB": step_gb, "gyB": step_gyb,
        "norm": step_norm, "part": step_part, "ryB": step_ryb, "rA": step_ra, "rB": step_rb,
        "tin": step_tin, "far": step_far, "tout": step_tout, "fl": step_fl, "fx": step_fx, "fy": step_fy, "fz": step_fz, "ft": step_ft, "pair": step_pair, "fin": step_fin,
        "ryA": step_rya, "endB": step_end_b, "endA": step_end_a,
    }
    for step in ORDER:
        steps[step[0]](*step[1:])

    for group in (0, 1):
        everything = w.at[pl.ds(0, sent[group] // (KC * 2))]
        pltpu.make_async_remote_copy(
            src_ref=everything, dst_ref=everything, send_sem=ssem.at[group], recv_sem=rsem.at[0],
            device_id=sdev, device_id_type=MESH,
        ).wait_send()


def store(*refs):
    n = (len(refs) - 1) // 2
    copies = [pltpu.make_async_copy(refs[i], refs[n + i], refs[-1].at[i]) for i in range(n)]
    for copy in copies:
        copy.start()
    for copy in copies:
        copy.wait()


def body(*args):
    outs = [
        ((1, TOK, KC), BF16),
        ((1, TOK, D), BF16),
        ((1, TOK, KC), F32),
        ((TOK, KC), F32),
        ((TOK, KC), F32),
        ((1, TOK, KC), BF16),
    ]
    vm = pltpu.VMEM
    results = pl.pallas_call(
        kernel,
        out_shape=[vm(*o) for o in outs],
        in_specs=[pl.BlockSpec(memory_space=pltpu.HBM)] * 7,
        out_specs=[pl.BlockSpec(memory_space=vm)] * 6,
        scratch_shapes=[
            vm((D, KC), BF16),
            vm((TOK, D), BF16),
            vm((2, TOK, D // 2), BF16),
            vm((TOK, D // 2), BF16),
            vm((TOK, D), F32),
            vm((NCHIP, KC, 256), F32),
            vm((1, D), BF16),
            vm((2, TOK, KC), BF16),
            vm((2, KC, TOK), BF16),
            vm((TOK, KC), F32),
            vm((TOK, 128), F32),
            vm((TOK, 1), F32),
            vm((TOK, KC), F32),
            vm((TOK, KC), F32),
            vm((TOK, KC), BF16),
            vm((3, 64, KC), BF16),
            vm((3, 64, KC), F32),
            vm((TOK, KC), F32),
            vm((2, 2, 4, RA, 256), BF16),
            vm((2, 2, RA, 256), BF16),
            vm((8, RB, 256), BF16),
            vm((8, RB, 256), BF16),
            vm((2, 4, RB, 256), BF16),
            vm((2, RB0, 256), BF16),
            vm((RA, 256), BF16),
            vm((RA, 256), BF16),
            pltpu.SemaphoreType.DMA((2,)),
            pltpu.SemaphoreType.DMA((len(ARRIVALS),)),
            pltpu.SemaphoreType.DMA((8,)),
            pltpu.SemaphoreType.REGULAR,
            pltpu.SemaphoreType.REGULAR,
            pltpu.SemaphoreType.REGULAR,
        ],
        compiler_params=pltpu.CompilerParams(
            collective_id=0, has_side_effects=True, vmem_limit_bytes=56 * 2**20
        ),
    )(*args)
    return tuple(
        pl.pallas_call(
            store,
            out_shape=[jax.ShapeDtypeStruct(*o) for o in outs],
            in_specs=[pl.BlockSpec(memory_space=pl.ANY)] * 6,
            out_specs=[pl.BlockSpec(memory_space=pl.ANY)] * 6,
            scratch_shapes=[pltpu.SemaphoreType.DMA((6,))],
            compiler_params=pltpu.CompilerParams(vmem_limit_bytes=2**20),
        )(*results)
    )


def solution(mesh):
    rows = P("island", "fsdp", None)
    frag = P("fsdp", None)
    return jax.shard_map(
        body,
        mesh=mesh,
        in_specs=(rows, P("island", None), rows, rows, frag, frag, rows),
        out_specs=(rows, rows, rows, frag, frag, rows),
        check_vma=False,
    )
```
